32 devices in a mesh: gx: 4 (over y, x), gy: 8 (over z, core).
Axes of the slice: x: 2, y: 2, z: 4, core: 2. Of those that a mesh axis runs over, the one named last changes fastest.
Arguments:
- hidden: bfloat16 [64, 2, 16384], P('gy', None, 'gx'), may hold values from -6 to 6
- norm_gain: bfloat16 [16384], P('gx'), may hold values from 0.5 to 1.5
- w_query: bfloat16 [16384, 16384], P('gx', 'gy'), may hold values from -0.046875 to 0.046875
- w_keyval: bfloat16 [2, 16384, 1024], P(None, 'gx', 'gy'), may hold values from -0.046875 to 0.046875
- w_out: bfloat16 [16384, 16384], P('gy', 'gx'), may hold values from -0.046875 to 0.046875
- cache_keys: bfloat16 [64, 1024, 1024], P(('gx', 'gy')), may hold values from -80 to 80, as said below
- cache_values: bfloat16 [64, 1024, 1024], P(('gx', 'gy')), may hold values from -16 to 16
- cache_lengths: int32 [64], P(('gx', 'gy')), may hold values from 1 to 1024, as said below
- positions: int32 [64], P(('gx', 'gy')), may hold values from 1 to 5119, as said below
Outputs:
- attn_branch: bfloat16 [64, 2, 16384], P('gy', None, 'gx')
- new_keyvals: bfloat16 [2, 64, 2, 1024], P(None, ('gx', 'gy'))
The draws below stay inside these ranges and needn't reach their ends.
Inputs may be any that keep to these rules, and one draw needn't show every extreme that they name: `cache_keys`: cached keys already carry their rotation. `cache_lengths`: some row has exactly 1024 valid slots and some row exactly 1. `positions`: each row's position is at least its cache length.
All inputs are finite; a program needn't handle non-finite values.
Results may differ from the reference program's by a relative error of at most 0.008.
The reference program's roundings to bfloat16 on the way count: a program that leaves them out, or rounds other values in their place, can miss the bound.
Values may be sent and summed in bfloat16 or wider, within the bound.
A program may use at most 128 MiB of HBM per device.

```python
import math
import jax
import jax.numpy as jnp
from jax import lax

D = 16384
HQ = 128
KVH = 8
HD = 128
STEPS = 2
S = 1024
B = 64


def row_draw(key):
    count_key, pick_key = jax.random.split(key)
    lengths = jax.random.randint(count_key, (B,), 1, S + 1)
    order = jax.random.permutation(pick_key, B)
    lengths = lengths.at[order[0]].set(S).at[order[1]].set(1)
    return (lengths.astype(jnp.int32), order)


def draw_cache_lengths(key, part):
    lengths, order = row_draw(key)
    return lengths


def draw_positions(key, part):
    lengths, order = row_draw(key)
    key = jax.random.fold_in(key, 7)
    offsets = jax.random.randint(key, (B,), 0, 4 * S)
    offsets = offsets.at[order[0]].set(4 * S - 1).at[order[1]].set(0)
    return (lengths + offsets).astype(jnp.int32)


def draw_cache_keys(key, part):
    lengths, order = row_draw(key)
    key = jax.random.fold_in(key, 11)
    noise_key = jax.random.fold_in(key, 0)
    sign_key = jax.random.fold_in(key, 2)
    slot_key = jax.random.fold_in(key, 3)
    level_key = jax.random.fold_in(key, 4)
    base = jnp.clip(jax.random.normal(noise_key, (B, S, KVH * HD), jnp.float32) * 1.5, -9.0, 9.0)
    row_rank = jnp.zeros((B,), jnp.int32).at[order].set(jnp.arange(B, dtype=jnp.int32))
    strong_rows = (row_rank == 0) | (row_rank >= 2) & (row_rank < 2 + B // 8)
    level_table = jnp.array([40.0, 60.0, 80.0], jnp.float32)
    strength = level_table[jax.random.randint(level_key, (B,), 0, 3)]
    strength = jnp.where(row_rank == 0, 80.0, strength)
    sign_pattern = (jax.random.randint(sign_key, (B, KVH * HD), 0, 2) * 2 - 1).astype(jnp.float32)
    first_slot = jax.random.randint(slot_key, (B,), 0, lengths)
    second_slot = (first_slot + 1) % lengths
    rows_index = jnp.arange(B)
    keep_second = base[rows_index, second_slot]
    new_second = jnp.where(strong_rows[:, None], 0.985 * strength[:, None] * sign_pattern, keep_second)
    base = base.at[rows_index, second_slot].set(new_second)
    keep_first = base[rows_index, first_slot]
    new_first = jnp.where(strong_rows[:, None], strength[:, None] * sign_pattern, keep_first)
    base = base.at[rows_index, first_slot].set(new_first)
    return base.astype(jnp.bfloat16)


def shard_levels(key, extent, cuts, smallest, largest):
    level, own = 1.0, jax.random.fold_in(key, 6)
    for position, blocks in cuts:
        draws = jnp.exp(jax.random.uniform(jax.random.fold_in(own, position), (blocks,), jnp.float32, smallest / len(cuts), largest / len(cuts)))
        level = level * jnp.repeat(draws, extent[position] // blocks).reshape([-1 if axis == position else 1 for axis in range(len(extent))])
    return level


def gaussian(key, dims, spread, limit, cuts=(), held_as=jnp.bfloat16):
    values = spread * jax.random.normal(key, dims, jnp.float32)
    if cuts:
        values = values * shard_levels(key, dims, cuts, -0.22, 0.18)
    return jnp.clip(values, -limit, limit).astype(held_as)


def setup_inputs(seed: int = 0) -> dict:
    arg_keys = jax.random.split(jax.random.key(seed), 10)
    return {
        "hidden": gaussian(arg_keys[0], (B, STEPS, D), 1.0, 6.0, ((0, 8), (2, 4))),
        "norm_gain": jnp.clip(1.0 + 0.1 * jax.random.normal(arg_keys[1], (D,), jnp.float32), 0.5, 1.5).astype(jnp.bfloat16),
        "w_query": gaussian(arg_keys[2], (D, HQ * HD), D ** -0.5, 0.046875, ((0, 4), (1, 8))),
        "w_keyval": gaussian(arg_keys[3], (2, D, KVH * HD), D ** -0.5, 0.046875, ((1, 4), (2, 8))),
        "w_out": gaussian(arg_keys[4], (HQ * HD, D), (HQ * HD) ** -0.5, 0.046875, ((0, 8), (1, 4))),
        "cache_keys": draw_cache_keys(jax.random.fold_in(arg_keys[9], 71), 0),
        "cache_values": gaussian(arg_keys[6], (B, S, KVH * HD), 4.0, 16.0, ((0, 32),)),
        "cache_lengths": draw_cache_lengths(jax.random.fold_in(arg_keys[9], 71), 0),
        "positions": draw_positions(jax.random.fold_in(arg_keys[9], 71), 0),
    }


norm_epsilon = 1e-05

def rope_rates():
    index = jnp.arange(HD // 2, dtype=jnp.float32)
    rates = 1.0 / jnp.power(500000.0, 2.0 * index / HD)
    wavelength = 2.0 * math.pi / rates
    smooth = (8192.0 / wavelength - 1.0) / 3.0
    blended = (1.0 - smooth) * rates / 8.0 + smooth * rates
    return jnp.where(wavelength > 8192.0, rates / 8.0, jnp.where(wavelength < 2048.0, rates, blended))

def rotate(vectors, places):
    angles = places[..., None, None] * rope_rates()
    half_size = vectors.shape[-1] // 2
    first_half = vectors[..., :half_size]
    second_half = vectors[..., half_size:]
    cosine = jnp.cos(angles)
    sine = jnp.sin(angles)
    return jnp.concatenate([first_half * cosine - second_half * sine, second_half * cosine + first_half * sine], axis=-1)

def attend(queries, fresh_keys, fresh_values, cached_keys, cached_values, lengths):
    rows, steps = (queries.shape[0], queries.shape[1])
    slots = cached_keys.shape[1]
    grouped = queries.reshape(rows, steps, KVH, HQ // KVH, HD).astype(jnp.float32)
    old_keys = cached_keys.reshape(rows, slots, KVH, HD).astype(jnp.float32)
    old_values = cached_values.reshape(rows, slots, KVH, HD).astype(jnp.float32)
    score_scale = HD ** (-0.5)
    cached = jnp.einsum('bskgd,btkd->bskgt', grouped, old_keys) * score_scale
    fresh = jnp.einsum('bskgd,brkd->bskgr', grouped, fresh_keys.astype(jnp.float32)) * score_scale
    slot_valid = jnp.arange(slots)[None, :] < lengths[:, None]
    step_valid = jnp.arange(steps)[None, :] <= jnp.arange(steps)[:, None]
    cached = jnp.where(slot_valid[:, None, None, None, :], cached, -1e+30)
    fresh = jnp.where(step_valid[None, :, None, None, :], fresh, -1e+30)
    highest = jnp.maximum(lax.optimization_barrier(jnp.max(cached, axis=-1)), lax.optimization_barrier(jnp.max(fresh, axis=-1)))[..., None]
    weights_old = jnp.exp(cached - highest)
    weights_new = jnp.exp(fresh - highest)
    denom = lax.optimization_barrier(jnp.sum(weights_old, axis=-1)) + lax.optimization_barrier(jnp.sum(weights_new, axis=-1))
    rounded_old = weights_old.astype(jnp.bfloat16).astype(jnp.float32)
    rounded_new = weights_new.astype(jnp.bfloat16).astype(jnp.float32)
    mixed = jnp.einsum('bskgt,btkd->bskgd', rounded_old, old_values)
    mixed = mixed + jnp.einsum('bskgr,brkd->bskgd', rounded_new, fresh_values.astype(jnp.float32))
    return (mixed / denom[..., None]).astype(jnp.bfloat16).reshape(rows, steps, HQ * HD)

def one_row(items):
    outcome = attend(items[0][None], items[1][None], items[2][None], items[3][None], items[4][None], items[5][None])
    return outcome[0]

def reference(hidden, norm_gain, w_query, w_keyval, w_out, cache_keys, cache_values, cache_lengths, positions):
    features = hidden.astype(jnp.float32)
    mean_square = lax.optimization_barrier(jnp.mean(features * features, axis=-1, keepdims=True))
    normed = (features * lax.rsqrt(mean_square + norm_epsilon) * norm_gain.astype(jnp.float32)).astype(jnp.bfloat16)
    rows, steps = (hidden.shape[0], hidden.shape[1])
    flattened = normed.reshape(rows * steps, D)
    queries = jnp.dot(flattened, w_query, preferred_element_type=jnp.float32).astype(jnp.bfloat16).reshape(rows, steps, HQ, HD)
    fresh_keys = jnp.dot(flattened, w_keyval[0], preferred_element_type=jnp.float32).astype(jnp.bfloat16).reshape(rows, steps, KVH, HD)
    fresh_values = jnp.dot(flattened, w_keyval[1], preferred_element_type=jnp.float32).astype(jnp.bfloat16).reshape(rows, steps, KVH, HD)
    places = positions.astype(jnp.float32)[:, None] + jnp.arange(steps, dtype=jnp.float32)[None, :]
    turned_queries = rotate(queries.astype(jnp.float32), places).astype(jnp.bfloat16)
    turned_keys = rotate(fresh_keys.astype(jnp.float32), places).astype(jnp.bfloat16)
    new_keyvals = jnp.stack([turned_keys.reshape(rows, steps, KVH * HD), fresh_values.reshape(rows, steps, KVH * HD)])
    attended = lax.map(one_row, (turned_queries, turned_keys, fresh_values, cache_keys, cache_values, cache_lengths))
    branch = jnp.dot(attended.reshape(rows * steps, HQ * HD), w_out, preferred_element_type=jnp.float32)
    return (branch.reshape(rows, steps, D).astype(jnp.bfloat16), new_keyvals)
```

```python
import functools
import math

import jax
import jax.numpy as jnp
from jax import lax
from jax.experimental import pallas as pl
from jax.experimental.pallas import tpu as pltpu
from jax.sharding import PartitionSpec as P

D = 16384
HQ = 128
KVH = 8
HD = 128
STEPS = 2


norm_epsilon = 1e-05


def rope_rates():
    index = jnp.arange(HD // 2, dtype=jnp.float32)
    rates = 1.0 / jnp.power(500000.0, 2.0 * index / HD)
    wavelength = 2.0 * math.pi / rates
    smooth = (8192.0 / wavelength - 1.0) / 3.0
    blended = (1.0 - smooth) * rates / 8.0 + smooth * rates
    return jnp.where(
        wavelength > 8192.0, rates / 8.0, jnp.where(wavelength < 2048.0, rates, blended)
    )


def rotate(vectors, places):
    angles = places[..., None, None] * rope_rates()
    half_size = vectors.shape[-1] // 2
    first_half = vectors[..., :half_size]
    second_half = vectors[..., half_size:]
    cosine = jnp.cos(angles)
    sine = jnp.sin(angles)
    return jnp.concatenate(
        [first_half * cosine - second_half * sine, second_half * cosine + first_half * sine],
        axis=-1,
    )


def attend(queries, fresh_keys, fresh_values, cached_keys, cached_values, lengths):
    rows, steps = (queries.shape[0], queries.shape[1])
    slots = cached_keys.shape[1]
    grouped = queries.reshape(rows, steps, KVH, HQ // KVH, HD)
    old_keys = cached_keys.reshape(rows, slots, KVH, HD)
    old_values = cached_values.reshape(rows, slots, KVH, HD)
    score_scale = HD ** (-0.5)
    cached = (
        jnp.einsum("bskgd,btkd->bskgt", grouped, old_keys, preferred_element_type=jnp.float32)
        * score_scale
    )
    fresh = (
        jnp.einsum("bskgd,brkd->bskgr", grouped, fresh_keys, preferred_element_type=jnp.float32)
        * score_scale
    )
    slot_valid = jnp.arange(slots)[None, :] < lengths[:, None]
    step_valid = jnp.arange(steps)[None, :] <= jnp.arange(steps)[:, None]
    cached = jnp.where(slot_valid[:, None, None, None, :], cached, -1e30)
    fresh = jnp.where(step_valid[None, :, None, None, :], fresh, -1e30)
    highest = jnp.maximum(jnp.max(cached, axis=-1), jnp.max(fresh, axis=-1))[..., None]
    weights_old = jnp.exp(cached - highest)
    weights_new = jnp.exp(fresh - highest)
    denom = jnp.sum(weights_old, axis=-1) + jnp.sum(weights_new, axis=-1)
    mixed = jnp.einsum(
        "bskgt,btkd->bskgd",
        weights_old.astype(jnp.bfloat16),
        old_values,
        preferred_element_type=jnp.float32,
    )
    mixed = mixed + jnp.einsum(
        "bskgr,brkd->bskgd",
        weights_new.astype(jnp.bfloat16),
        fresh_values,
        preferred_element_type=jnp.float32,
    )
    return (mixed / denom[..., None]).astype(jnp.bfloat16).reshape(rows, steps, HQ * HD)


def plain(
    hidden, norm_gain, w_query, w_keyval, w_out, cache_keys, cache_values, cache_lengths, positions
):
    steps = hidden.shape[1]
    features = hidden.astype(jnp.float32)
    squares = jnp.sum(features * features, axis=-1)
    square_sums = lax.psum(squares, "gx")
    inverse = lax.rsqrt(square_sums / D + norm_epsilon)
    normed = (features * inverse[..., None] * norm_gain.astype(jnp.float32)).astype(jnp.bfloat16)
    shard_rows = lax.all_gather(normed, "gy", axis=0, tiled=True)
    flattened = shard_rows.reshape(-1, shard_rows.shape[2])
    products = [
        jnp.dot(flattened, w_query, preferred_element_type=jnp.float32),
        jnp.dot(flattened, w_keyval[0], preferred_element_type=jnp.float32),
        jnp.dot(flattened, w_keyval[1], preferred_element_type=jnp.float32),
    ]
    partial_sums = jnp.concatenate(products, axis=-1).reshape(shard_rows.shape[0], steps, -1)
    width_parts = lax.axis_size("gx")
    head_parts = lax.axis_size("gy")
    block_rows = partial_sums.shape[0] // width_parts
    summed = lax.psum(partial_sums, "gx")
    summed = lax.dynamic_slice_in_dim(summed, lax.axis_index("gx") * block_rows, block_rows, 0)
    own_rows = summed.astype(jnp.bfloat16)
    arrived = lax.all_to_all(own_rows, "gy", split_axis=0, concat_axis=2, tiled=True)
    local_rows = arrived.shape[0]
    pieces = arrived.reshape(local_rows, steps, head_parts, -1)
    query_cols = w_query.shape[1]
    keyval_cols = w_keyval.shape[2]
    queries = pieces[..., :query_cols].reshape(local_rows, steps, HQ, HD)
    fresh_keys = pieces[..., query_cols : query_cols + keyval_cols].reshape(
        local_rows, steps, KVH, HD
    )
    fresh_values = pieces[..., query_cols + keyval_cols :].reshape(local_rows, steps, KVH, HD)
    places = positions.astype(jnp.float32)[:, None] + jnp.arange(steps, dtype=jnp.float32)[None, :]
    turned_queries = rotate(queries.astype(jnp.float32), places).astype(jnp.bfloat16)
    turned_keys = rotate(fresh_keys.astype(jnp.float32), places).astype(jnp.bfloat16)
    new_keyvals = jnp.stack(
        [
            turned_keys.reshape(local_rows, steps, KVH * HD),
            fresh_values.reshape(local_rows, steps, KVH * HD),
        ]
    )
    attended = attend(
        turned_queries, turned_keys, fresh_values, cache_keys, cache_values, cache_lengths
    )
    returned = lax.all_to_all(attended, "gy", split_axis=2, concat_axis=0, tiled=True)
    rows_all = lax.all_gather(returned, "gx", axis=0, tiled=True)
    head_cols = rows_all.shape[2]
    all_rows = rows_all.shape[0]
    out_rows_here = all_rows // head_parts
    product = jnp.dot(
        rows_all.reshape(lax.axis_size("gy") * out_rows_here * steps, head_cols),
        w_out,
        preferred_element_type=jnp.float32,
    )
    branch = lax.psum_scatter(
        product.reshape(lax.axis_size("gy") * out_rows_here, steps, -1),
        "gy",
        scatter_dimension=0,
        tiled=True,
    )
    return (branch.astype(jnp.bfloat16), new_keyvals)


def peer_id(axis, index):
    return {axis: index}


def remote(src, dst, send_sem, recv_sem, axis, index):
    return pltpu.make_async_remote_copy(
        src_ref=src,
        dst_ref=dst,
        send_sem=send_sem,
        recv_sem=recv_sem,
        device_id=peer_id(axis, index),
        device_id_type=pl.DeviceIdType.MESH,
    )


def greet(x, y, nx, ny):
    barrier = pltpu.get_barrier_semaphore()
    for d in range(1, nx):
        pl.semaphore_signal(
            barrier, inc=1, device_id=peer_id("gx", lax.rem(x + d, nx)),
            device_id_type=pl.DeviceIdType.MESH,
        )
    for d in range(1, ny):
        pl.semaphore_signal(
            barrier, inc=1, device_id=peer_id("gy", lax.rem(y + d, ny)),
            device_id_type=pl.DeviceIdType.MESH,
        )
    pl.semaphore_wait(barrier, nx - 1 + ny - 1)


def project_kernel(
    nx, ny, x_ref, gain_ref, wq_hbm, wkv_hbm, out_ref,
    wq, wkv, xbuf, sqbuf, parts, rbuf, qbuf, kvbuf, sendbuf, landed,
    wq_sem, wkv_sem, sq_s, sq_r, g_s, g_r, rs_s, rs_r, a_s, a_r,
):
    x = lax.axis_index("gx")
    y = lax.axis_index("gy")
    nz = ny // 2
    z = y // 2
    c = lax.rem(y, 2)
    nblocks = wq.shape[0]
    bc = wq.shape[2]
    head = wkv.shape[2]
    chunk = rbuf.shape[2]

    def load_q(j):
        cols = pl.ds(j * bc, bc) if isinstance(j, int) else pl.ds(pl.multiple_of(j * bc, bc), bc)
        return pltpu.make_async_copy(wq_hbm.at[:, cols], wq.at[j], wq_sem.at[j])

    def load_kv():
        return pltpu.make_async_copy(wkv_hbm, wkv, wkv_sem)

    load_kv().start()
    for j in range(nblocks):
        load_q(j).start()

    features = x_ref[...].astype(jnp.float32)
    squares = jnp.sum(features * features, axis=-1, keepdims=True)
    sqbuf[0] = jnp.broadcast_to(squares, sqbuf.shape[1:])
    greet(x, y, nx, ny)
    sq_copies = [
        remote(sqbuf.at[0], sqbuf.at[d], sq_s.at[d - 1], sq_r.at[d - 1], "gx", lax.rem(x + d, nx))
        for d in range(1, nx)
    ]
    for copy in sq_copies:
        copy.start()
    for copy in sq_copies:
        copy.wait_recv()
    total = sqbuf[0]
    for d in range(1, nx):
        total = total + sqbuf[d]
    inverse = lax.rsqrt(total[:, :1] / D + norm_epsilon)
    xbuf[y] = (features * inverse * gain_ref[...].astype(jnp.float32)).astype(jnp.bfloat16)

    def hop(block, k):
        dest = (y - 2, y + 2, y + 1 - 2 * c)[k]
        return remote(xbuf.at[block], xbuf.at[block], g_s.at[block, k], g_r.at[block], "gy", dest)

    @pl.when(z > 0)
    def _():
        hop(y, 0).start()

    @pl.when(z < nz - 1)
    def _():
        hop(y, 1).start()

    hop(y, 2).start()
    for d in range(1, nz):

        @pl.when(z - d >= 0)
        def _():
            block = y - 2 * d
            hop(block, 2).wait_recv()

            @pl.when(z < nz - 1)
            def _():
                hop(block, 1).start()

            hop(block, 2).start()

        @pl.when(z + d < nz)
        def _():
            block = y + 2 * d
            hop(block, 2).wait_recv()

            @pl.when(z > 0)
            def _():
                hop(block, 0).start()

            hop(block, 2).start()

    for zz in range(nz):
        hop(2 * zz + 1 - c, 2).wait_recv()

    def rs(j, d):
        to = lax.rem(x + d, nx)
        rows = pl.ds(pl.multiple_of(to * chunk, chunk), chunk)
        return remote(
            parts.at[j, rows, :], rbuf.at[d - 1, j], rs_s.at[d - 1, j], rs_r.at[d - 1, j], "gx", to
        )

    tokens = xbuf.shape[0] * xbuf.shape[1]
    load_kv().wait()
    for n in range(2):
        parts[nblocks, :, n * head : (n + 1) * head] = jnp.dot(
            xbuf[...].reshape(tokens, xbuf.shape[2]), wkv[n], preferred_element_type=jnp.float32
        )
    for d in range(1, nx):
        rs(nblocks, d).start()

    def block_step(j, carry):
        load_q(j).wait()
        parts[j] = jnp.dot(
            xbuf[...].reshape(tokens, xbuf.shape[2]), wq[j], preferred_element_type=jnp.float32
        )
        for d in range(1, nx):
            rs(j, d).start()
        return carry

    lax.fori_loop(0, nblocks, block_step, 0)

    own = pl.ds(pl.multiple_of(x * chunk, chunk), chunk)
    per_block = bc // head
    heads = nblocks * per_block
    kvbuf[...] = jnp.zeros_like(kvbuf)
    for j in [nblocks] + list(range(nblocks)):
        for d in range(1, nx):
            rs(j, d).wait_recv()
        summed = parts[j, own, :]
        for d in range(1, nx):
            summed = summed + rbuf[d - 1, j]
        for i in range(per_block):
            piece = summed[:, i * head : (i + 1) * head]
            if j < nblocks:
                qbuf[pl.ds(j * per_block + i, chunk, stride=heads), :] = piece
            else:
                kvbuf[pl.ds(i, chunk, stride=4), :] = piece
    local = chunk // ny
    sendbuf[:, : local * heads, :] = (
        qbuf[...].astype(jnp.bfloat16).reshape(ny, local * heads, head)
    )
    sendbuf[:, local * heads :, :] = kvbuf[...].astype(jnp.bfloat16).reshape(ny, local * 4, head)

    def a2a(d):
        to = lax.rem(y + d, ny)
        return remote(sendbuf.at[to], landed.at[y], a_s.at[d - 1], a_r.at[d - 1], "gy", to)

    for d in range(1, ny):
        a2a(d).start()
    landed[y] = sendbuf[y]
    for d in range(1, ny):
        a2a(d).wait_recv()
    out_ref[...] = landed[...]

    for copy in sq_copies:
        copy.wait_send()
    for zz in range(nz):
        block = 2 * zz + c
        hop(block, 2).wait_send()

        @pl.when((zz >= z) & (z > 0))
        def _():
            hop(block, 0).wait_send()

        @pl.when((zz <= z) & (z < nz - 1))
        def _():
            hop(block, 1).wait_send()

    def rs_done(j, carry):
        for d in range(1, nx):
            rs(j, d).wait_send()
        return carry

    lax.fori_loop(0, nblocks + 1, rs_done, 0)
    for d in range(1, ny):
        a2a(d).wait_send()


def attend_kernel(len_ref, x_ref, cos_ref, sin_ref, key_ref, val_ref, out_ref, kv_ref):
    rows = key_ref.shape[0]
    slots = key_ref.shape[1]
    head = key_ref.shape[2]
    steps = STEPS
    group = (x_ref.shape[1] // rows - 4 * steps) // steps
    nq = steps * group
    scale = HD ** (-0.5)
    raw = x_ref[0].astype(jnp.float32)
    swapped = jnp.concatenate([raw[:, head // 2 :], raw[:, : head // 2]], axis=1)
    turned = (raw * cos_ref[...] + swapped * sin_ref[...]).astype(jnp.bfloat16)
    turned_f = turned.astype(jnp.float32)
    col = lax.broadcasted_iota(jnp.int32, (nq, 4 * steps), 1)
    step = lax.broadcasted_iota(jnp.int32, (nq, 4 * steps), 0) // group
    keep_new = (col % 4 == 0) & (col // 4 <= step)
    slot = lax.broadcasted_iota(jnp.int32, (nq, slots), 1)
    keys_out, values_out = [], []
    for b in range(rows):
        q = turned[b * nq : (b + 1) * nq]
        base = rows * nq + b * 4 * steps
        kv_turned = turned_f[base : base + 4 * steps]
        kv_raw = raw[base : base + 4 * steps]
        old = lax.dot_general(
            q, key_ref[b], (((1,), (1,)), ((), ())), preferred_element_type=jnp.float32
        ) * scale
        new = lax.dot_general(
            q, kv_turned.astype(jnp.bfloat16), (((1,), (1,)), ((), ())),
            preferred_element_type=jnp.float32,
        ) * scale
        old = jnp.where(slot < len_ref[b], old, -1e30)
        new = jnp.where(keep_new, new, -1e30)
        highest = jnp.maximum(
            jnp.max(old, axis=-1, keepdims=True), jnp.max(new, axis=-1, keepdims=True)
        )
        old = jnp.exp(old - highest)
        new = jnp.exp(new - highest)
        denom = jnp.sum(old, axis=-1, keepdims=True) + jnp.sum(new, axis=-1, keepdims=True)
        mixed = jnp.dot(old.astype(jnp.bfloat16), val_ref[b], preferred_element_type=jnp.float32)
        new = new.astype(jnp.bfloat16).astype(jnp.float32)
        for r in range(steps):
            mixed = mixed + new[:, 4 * r : 4 * r + 1] * kv_raw[4 * r + 1 : 4 * r + 2]
            keys_out.append(kv_turned[4 * r : 4 * r + 1])
            values_out.append(kv_raw[4 * r + 1 : 4 * r + 2])
        out_ref[0, b * nq : (b + 1) * nq] = (mixed / denom).astype(jnp.bfloat16)
    kv_ref[...] = jnp.concatenate(keys_out + values_out, axis=0)


def output_kernel(
    nx, ny, att_ref, wo_hbm, out_ref,
    wo, abuf, fbuf, lbuf, prod, sbuf, rbuf, chip, zsend, zland,
    wo_sem, a_s, a_r, g_s, g_r, c_s, c_r, z_s, z_r,
):
    x = lax.axis_index("gx")
    y = lax.axis_index("gy")
    nz = ny // 2
    z = y // 2
    c = lax.rem(y, 2)
    nblocks = wo.shape[0]
    bc = wo.shape[2]

    def load(j):
        cols = pl.ds(j * bc, bc) if isinstance(j, int) else pl.ds(pl.multiple_of(j * bc, bc), bc)
        return pltpu.make_async_copy(wo_hbm.at[:, cols], wo.at[j], wo_sem.at[j])

    for j in range(nblocks):
        load(j).start()
    greet(x, y, nx, ny)

    def a2a(d):
        to = lax.rem(y + d, ny)
        return remote(att_ref.at[to], abuf.at[y], a_s.at[d - 1], a_r.at[d - 1], "gy", to)

    for d in range(1, ny):
        a2a(d).start()
    abuf[y] = att_ref[y]
    for d in range(1, ny):
        a2a(d).wait_recv()
    head = abuf.shape[2]
    chunk = lbuf.shape[1]
    heads = lbuf.shape[2] // head
    fbuf[...] = abuf[...].astype(jnp.float32).reshape(fbuf.shape)
    for h in range(heads):
        lbuf[x, :, h * head : (h + 1) * head] = fbuf[
            pl.ds(h, chunk, stride=heads), :
        ].astype(jnp.bfloat16)

    def gather(d):
        return remote(
            lbuf.at[x], lbuf.at[x], g_s.at[d - 1], g_r.at[d - 1], "gx", lax.rem(x + d, nx)
        )

    for d in range(1, nx):
        gather(d).start()
    for d in range(1, nx):
        gather(d).wait_recv()

    def pair(j):
        return remote(sbuf.at[j], rbuf.at[j], c_s.at[j], c_r.at[j], "gy", y + 1 - 2 * c)

    def along(j, d):
        to = lax.rem(z + d, nz)
        return remote(
            zsend.at[j, to], zland.at[d - 1, j], z_s.at[d - 1, j], z_r.at[d - 1, j], "gy", 2 * to + c
        )

    def pass_on(j):
        pair(j).wait_recv()
        chip[j] = prod[j, :, c] + rbuf[j].astype(jnp.float32)
        zsend[j] = chip[j].astype(jnp.bfloat16)
        for d in range(1, nz):
            along(j, d).start()

    def block_step(j, carry):
        load(j).wait()
        prod[j] = jnp.dot(
            lbuf[...].reshape(nx * chunk, lbuf.shape[2]), wo[j], preferred_element_type=jnp.float32
        ).reshape(prod.shape[1:])
        sbuf[j] = prod[j, :, 1 - c].astype(jnp.bfloat16)
        pair(j).start()

        @pl.when(j > 0)
        def _():
            pass_on(j - 1)

        return carry

    lax.fori_loop(0, nblocks, block_step, 0)
    pass_on(nblocks - 1)
    for j in range(nblocks):
        total = chip[j, z]
        for d in range(1, nz):
            along(j, d).wait_recv()
            total = total + zland[d - 1, j].astype(jnp.float32)
        out_ref[:, j * bc : (j + 1) * bc] = total.astype(jnp.bfloat16)

    for d in range(1, ny):
        a2a(d).wait_send()
    for d in range(1, nx):
        gather(d).wait_send()

    def done(j, carry):
        pair(j).wait_send()
        for d in range(1, nz):
            along(j, d).wait_send()
        return carry

    lax.fori_loop(0, nblocks, done, 0)


def with_kernels(
    hidden, norm_gain, w_query, w_keyval, w_out, cache_keys, cache_values, cache_lengths, positions
):
    nx = lax.axis_size("gx")
    ny = lax.axis_size("gy")
    nz = ny // 2
    rows, steps, width = hidden.shape
    mine = rows * steps
    tokens = ny * mine
    chunk = tokens // nx
    local_rows = cache_keys.shape[0]
    local = local_rows * steps
    cols = w_query.shape[1]
    heads = cols // HD
    bc = 256
    nq = cols // bc
    packed = local * heads + local * 4
    vmem = pl.BlockSpec(memory_space=pltpu.VMEM)
    hbm = pl.BlockSpec(memory_space=pl.ANY)
    dma = pltpu.SemaphoreType.DMA
    arrived = pl.pallas_call(
        functools.partial(project_kernel, nx, ny),
        out_shape=jax.ShapeDtypeStruct((ny, packed, HD), jnp.bfloat16),
        in_specs=[vmem, vmem, hbm, hbm],
        out_specs=vmem,
        scratch_shapes=[
            pltpu.VMEM((nq, width, bc), jnp.bfloat16),
            pltpu.VMEM(w_keyval.shape, jnp.bfloat16),
            pltpu.VMEM((ny, mine, width), jnp.bfloat16),
            pltpu.VMEM((nx, mine, 128), jnp.float32),
            pltpu.VMEM((nq + 1, tokens, bc), jnp.float32),
            pltpu.VMEM((nx - 1, nq + 1, chunk, bc), jnp.float32),
            pltpu.VMEM((chunk * heads, HD), jnp.float32),
            pltpu.VMEM((chunk * 4, HD), jnp.float32),
            pltpu.VMEM((ny, packed, HD), jnp.bfloat16),
            pltpu.VMEM((ny, packed, HD), jnp.bfloat16),
            dma((nq,)),
            dma(()),
            dma((nx - 1,)),
            dma((nx - 1,)),
            dma((ny, 3)),
            dma((ny,)),
            dma((nx - 1, nq + 1)),
            dma((nx - 1, nq + 1)),
            dma((ny - 1,)),
            dma((ny - 1,)),
        ],
        compiler_params=pltpu.CompilerParams(
            collective_id=0, has_side_effects=True, vmem_limit_bytes=48 * 1024 * 1024
        ),
        name="project",
    )(hidden.reshape(mine, width), norm_gain.reshape(1, width), w_query, w_keyval)

    places = positions.astype(jnp.float32)[:, None] + jnp.arange(steps, dtype=jnp.float32)[None, :]
    angles = places.reshape(local, 1) * rope_rates()[None, :]
    cosine, sine = jnp.cos(angles), jnp.sin(angles)
    cosine = jnp.concatenate([cosine, cosine], axis=-1)
    sine = jnp.concatenate([-sine, sine], axis=-1)
    spread = lambda table: jnp.concatenate(
        [jnp.repeat(table, heads, axis=0), jnp.repeat(table, 4, axis=0)], axis=0
    )
    slots = cache_keys.shape[1]
    attended, new = pl.pallas_call(
        attend_kernel,
        grid=(ny,),
        out_shape=(
            jax.ShapeDtypeStruct((ny, local * heads, HD), jnp.bfloat16),
            jax.ShapeDtypeStruct((2 * local, KVH * HD), jnp.float32),
        ),
        in_specs=[
            pl.BlockSpec(memory_space=pltpu.SMEM),
            pl.BlockSpec((1, packed, HD), lambda g: (g, 0, 0)),
            pl.BlockSpec((packed, HD), lambda g: (0, 0)),
            pl.BlockSpec((packed, HD), lambda g: (0, 0)),
            pl.BlockSpec((local_rows, slots, HD), lambda g: (0, 0, g)),
            pl.BlockSpec((local_rows, slots, HD), lambda g: (0, 0, g)),
        ],
        out_specs=(
            pl.BlockSpec((1, local * heads, HD), lambda g: (g, 0, 0)),
            pl.BlockSpec((2 * local, HD), lambda g: (0, g)),
        ),
        compiler_params=pltpu.CompilerParams(vmem_limit_bytes=32 * 1024 * 1024),
        name="attend",
    )(cache_lengths, arrived, spread(cosine), spread(sine), cache_keys, cache_values)
    new_keyvals = new.astype(jnp.bfloat16).reshape(2, local_rows, steps, KVH * HD)

    oc = 512
    no = w_out.shape[1] // oc
    branch = pl.pallas_call(
        functools.partial(output_kernel, nx, ny),
        out_shape=jax.ShapeDtypeStruct((mine, w_out.shape[1]), jnp.bfloat16),
        in_specs=[vmem, hbm],
        out_specs=vmem,
        scratch_shapes=[
            pltpu.VMEM((no, cols, oc), jnp.bfloat16),
            pltpu.VMEM((ny, local * heads, HD), jnp.bfloat16),
            pltpu.VMEM((chunk * heads, HD), jnp.float32),
            pltpu.VMEM((nx, chunk, cols), jnp.bfloat16),
            pltpu.VMEM((no, nz, 2, mine, oc), jnp.float32),
            pltpu.VMEM((no, nz, mine, oc), jnp.bfloat16),
            pltpu.VMEM((no, nz, mine, oc), jnp.bfloat16),
            pltpu.VMEM((no, nz, mine, oc), jnp.float32),
            pltpu.VMEM((no, nz, mine, oc), jnp.bfloat16),
            pltpu.VMEM((nz - 1, no, mine, oc), jnp.bfloat16),
            dma((no,)),
            dma((ny - 1,)),
            dma((ny - 1,)),
            dma((nx - 1,)),
            dma((nx - 1,)),
            dma((no,)),
            dma((no,)),
            dma((nz - 1, no)),
            dma((nz - 1, no)),
        ],
        compiler_params=pltpu.CompilerParams(
            collective_id=1, has_side_effects=True, vmem_limit_bytes=48 * 1024 * 1024
        ),
        name="output",
    )(attended, w_out)
    return (branch.reshape(rows, steps, -1), new_keyvals)


def on_device(*args):
    hidden, _, w_query, w_keyval, w_out, cache_keys = args[:6]
    nx, ny = lax.axis_size("gx"), lax.axis_size("gy")
    local = cache_keys.shape[0] * hidden.shape[1]
    fits = (
        w_keyval.shape[2] == HD
        and ny == KVH
        and hidden.shape[1] == STEPS
        and hidden.shape[0] * hidden.shape[1] % 16 == 0
        and local == 4
        and w_query.shape[1] % 256 == 0
        and w_out.shape[1] % 512 == 0
        and nx > 1
    )
    return with_kernels(*args) if fits else plain(*args)


def solution(mesh):
    return jax.shard_map(
        on_device,
        mesh=mesh,
        in_specs=(
            P("gy", None, "gx"),
            P("gx"),
            P("gx", "gy"),
            P(None, "gx", "gy"),
            P("gy", "gx"),
            P(("gx", "gy"), None, None),
            P(("gx", "gy"), None, None),
            P(("gx", "gy")),
            P(("gx", "gy")),
        ),
        out_specs=(P("gy", None, "gx"), P(None, ("gx", "gy"), None, None)),
        check_vma=False,
    )
```

```python
import functools
import math

import jax
import jax.numpy as jnp
from jax import lax
from jax.experimental import pallas as pl
from jax.experimental.pallas import tpu as pltpu
from jax.sharding import PartitionSpec as P

D = 16384
HQ = 128
KVH = 8
HD = 128
STEPS = 2


norm_epsilon = 1e-05


def rope_rates():
    index = jnp.arange(HD // 2, dtype=jnp.float32)
    rates = 1.0 / jnp.power(500000.0, 2.0 * index / HD)
    wavelength = 2.0 * math.pi / rates
    smooth = (8192.0 / wavelength - 1.0) / 3.0
    blended = (1.0 - smooth) * rates / 8.0 + smooth * rates
    return jnp.where(
        wavelength > 8192.0, rates / 8.0, jnp.where(wavelength < 2048.0, rates, blended)
    )


def rotate(vectors, places):
    angles = places[..., None, None] * rope_rates()
    half_size = vectors.shape[-1] // 2
    first_half = vectors[..., :half_size]
    second_half = vectors[..., half_size:]
    cosine = jnp.cos(angles)
    sine = jnp.sin(angles)
    return jnp.concatenate(
        [first_half * cosine - second_half * sine, second_half * cosine + first_half * sine],
        axis=-1,
    )


def attend(queries, fresh_keys, fresh_values, cached_keys, cached_values, lengths):
    rows, steps = (queries.shape[0], queries.shape[1])
    slots = cached_keys.shape[1]
    grouped = queries.reshape(rows, steps, KVH, HQ // KVH, HD)
    old_keys = cached_keys.reshape(rows, slots, KVH, HD)
    old_values = cached_values.reshape(rows, slots, KVH, HD)
    score_scale = HD ** (-0.5)
    cached = (
        jnp.einsum("bskgd,btkd->bskgt", grouped, old_keys, preferred_element_type=jnp.float32)
        * score_scale
    )
    fresh = (
        jnp.einsum("bskgd,brkd->bskgr", grouped, fresh_keys, preferred_element_type=jnp.float32)
        * score_scale
    )
    slot_valid = jnp.arange(slots)[None, :] < lengths[:, None]
    step_valid = jnp.arange(steps)[None, :] <= jnp.arange(steps)[:, None]
    cached = jnp.where(slot_valid[:, None, None, None, :], cached, -1e30)
    fresh = jnp.where(step_valid[None, :, None, None, :], fresh, -1e30)
    highest = jnp.maximum(jnp.max(cached, axis=-1), jnp.max(fresh, axis=-1))[..., None]
    weights_old = jnp.exp(cached - highest)
    weights_new = jnp.exp(fresh - highest)
    denom = jnp.sum(weights_old, axis=-1) + jnp.sum(weights_new, axis=-1)
    mixed = jnp.einsum(
        "bskgt,btkd->bskgd",
        weights_old.astype(jnp.bfloat16),
        old_values,
        preferred_element_type=jnp.float32,
    )
    mixed = mixed + jnp.einsum(
        "bskgr,brkd->bskgd",
        weights_new.astype(jnp.bfloat16),
        fresh_values,
        preferred_element_type=jnp.float32,
    )
    return (mixed / denom[..., None]).astype(jnp.bfloat16).reshape(rows, steps, HQ * HD)


def plain(
    hidden, norm_gain, w_query, w_keyval, w_out, cache_keys, cache_values, cache_lengths, positions
):
    steps = hidden.shape[1]
    features = hidden.astype(jnp.float32)
    squares = jnp.sum(features * features, axis=-1)
    square_sums = lax.psum(squares, "gx")
    inverse = lax.rsqrt(square_sums / D + norm_epsilon)
    normed = (features * inverse[..., None] * norm_gain.astype(jnp.float32)).astype(jnp.bfloat16)
    shard_rows = lax.all_gather(normed, "gy", axis=0, tiled=True)
    flattened = shard_rows.reshape(-1, shard_rows.shape[2])
    products = [
        jnp.dot(flattened, w_query, preferred_element_type=jnp.float32),
        jnp.dot(flattened, w_keyval[0], preferred_element_type=jnp.float32),
        jnp.dot(flattened, w_keyval[1], preferred_element_type=jnp.float32),
    ]
    partial_sums = jnp.concatenate(products, axis=-1).reshape(shard_rows.shape[0], steps, -1)
    width_parts = lax.axis_size("gx")
    head_parts = lax.axis_size("gy")
    block_rows = partial_sums.shape[0] // width_parts
    summed = lax.psum(partial_sums, "gx")
    summed = lax.dynamic_slice_in_dim(summed, lax.axis_index("gx") * block_rows, block_rows, 0)
    own_rows = summed.astype(jnp.bfloat16)
    arrived = lax.all_to_all(own_rows, "gy", split_axis=0, concat_axis=2, tiled=True)
    local_rows = arrived.shape[0]
    pieces = arrived.reshape(local_rows, steps, head_parts, -1)
    query_cols = w_query.shape[1]
    keyval_cols = w_keyval.shape[2]
    queries = pieces[..., :query_cols].reshape(local_rows, steps, HQ, HD)
    fresh_keys = pieces[..., query_cols : query_cols + keyval_cols].reshape(
        local_rows, steps, KVH, HD
    )
    fresh_values = pieces[..., query_cols + keyval_cols :].reshape(local_rows, steps, KVH, HD)
    places = positions.astype(jnp.float32)[:, None] + jnp.arange(steps, dtype=jnp.float32)[None, :]
    turned_queries = rotate(queries.astype(jnp.float32), places).astype(jnp.bfloat16)
    turned_keys = rotate(fresh_keys.astype(jnp.float32), places).astype(jnp.bfloat16)
    new_keyvals = jnp.stack(
        [
            turned_keys.reshape(local_rows, steps, KVH * HD),
            fresh_values.reshape(local_rows, steps, KVH * HD),
        ]
    )
    attended = attend(
        turned_queries, turned_keys, fresh_values, cache_keys, cache_values, cache_lengths
    )
    returned = lax.all_to_all(attended, "gy", split_axis=2, concat_axis=0, tiled=True)
    rows_all = lax.all_gather(returned, "gx", axis=0, tiled=True)
    head_cols = rows_all.shape[2]
    all_rows = rows_all.shape[0]
    out_rows_here = all_rows // head_parts
    product = jnp.dot(
        rows_all.reshape(lax.axis_size("gy") * out_rows_here * steps, head_cols),
        w_out,
        preferred_element_type=jnp.float32,
    )
    branch = lax.psum_scatter(
        product.reshape(lax.axis_size("gy") * out_rows_here, steps, -1),
        "gy",
        scatter_dimension=0,
        tiled=True,
    )
    return (branch.astype(jnp.bfloat16), new_keyvals)


def peer_id(axis, index):
    return {axis: index}


def remote(src, dst, send_sem, recv_sem, axis, index):
    return pltpu.make_async_remote_copy(
        src_ref=src,
        dst_ref=dst,
        send_sem=send_sem,
        recv_sem=recv_sem,
        device_id=peer_id(axis, index),
        device_id_type=pl.DeviceIdType.MESH,
    )


def greet(x, y, nx, ny):
    barrier = pltpu.get_barrier_semaphore()
    for d in range(1, nx):
        pl.semaphore_signal(
            barrier, inc=1, device_id=peer_id("gx", lax.rem(x + d, nx)),
            device_id_type=pl.DeviceIdType.MESH,
        )
    for d in range(1, ny):
        pl.semaphore_signal(
            barrier, inc=1, device_id=peer_id("gy", lax.rem(y + d, ny)),
            device_id_type=pl.DeviceIdType.MESH,
        )
    pl.semaphore_wait(barrier, nx - 1 + ny - 1)


def layer_kernel(
    nx, ny, x_ref, gain_ref, len_ref, cos_ref, sin_ref, wq_hbm, wkv_hbm, key_hbm, val_hbm, wo_hbm,
    out_ref, kv_ref,
    wq, wkv, xbuf, sqbuf, parts, rbuf, qbuf, kvbuf, sendbuf, landed,
    keys, vals, wo, att, abuf, fbuf, lbuf, prod, pbuf, qland, chip, zsend, zland,
    wq_sem, wkv_sem, sq_s, sq_r, g_s, g_r, rs_s, rs_r, a_s, a_r,
    key_sem, val_sem, wo_sem, b_s, b_r, l_s, l_r, c_s, c_r, z_s, z_r,
):
    x = lax.axis_index("gx")
    y = lax.axis_index("gy")
    nz = ny // 2
    z = y // 2
    c = lax.rem(y, 2)
    nblocks = wq.shape[0]
    bc = wq.shape[2]
    head = wkv.shape[2]
    chunk = rbuf.shape[2]
    no = wo.shape[0]
    oc = wo.shape[2]

    def load_q(j):
        cols = pl.ds(j * bc, bc) if isinstance(j, int) else pl.ds(pl.multiple_of(j * bc, bc), bc)
        return pltpu.make_async_copy(wq_hbm.at[:, cols], wq.at[j], wq_sem.at[j])

    def load_kv():
        return pltpu.make_async_copy(wkv_hbm, wkv, wkv_sem)

    load_kv().start()
    for j in range(nblocks):
        load_q(j).start()

    features = x_ref[...].astype(jnp.float32)
    squares = jnp.sum(features * features, axis=-1, keepdims=True)
    sqbuf[0] = jnp.broadcast_to(squares, sqbuf.shape[1:])
    greet(x, y, nx, ny)
    sq_copies = [
        remote(sqbuf.at[0], sqbuf.at[d], sq_s.at[d - 1], sq_r.at[d - 1], "gx", lax.rem(x + d, nx))
        for d in range(1, nx)
    ]
    for copy in sq_copies:
        copy.start()
    for copy in sq_copies:
        copy.wait_recv()
    total = sqbuf[0]
    for d in range(1, nx):
        total = total + sqbuf[d]
    inverse = lax.rsqrt(total[:, :1] / D + norm_epsilon)
    xbuf[y] = (features * inverse * gain_ref[...].astype(jnp.float32)).astype(jnp.bfloat16)

    def hop(block, k):
        dest = (y - 2, y + 2, y + 1 - 2 * c)[k]
        return remote(xbuf.at[block], xbuf.at[block], g_s.at[block, k], g_r.at[block], "gy", dest)

    @pl.when(z > 0)
    def _():
        hop(y, 0).start()

    @pl.when(z < nz - 1)
    def _():
        hop(y, 1).start()

    hop(y, 2).start()
    for d in range(1, nz):

        @pl.when(z - d >= 0)
        def _():
            block = y - 2 * d
            hop(block, 2).wait_recv()

            @pl.when(z < nz - 1)
            def _():
                hop(block, 1).start()

            hop(block, 2).start()

        @pl.when(z + d < nz)
        def _():
            block = y + 2 * d
            hop(block, 2).wait_recv()

            @pl.when(z > 0)
            def _():
                hop(block, 0).start()

            hop(block, 2).start()

    for zz in range(nz):
        hop(2 * zz + 1 - c, 2).wait_recv()

    def load_cache(g):
        cols = pl.ds(g * head, head) if isinstance(g, int) else pl.ds(pl.multiple_of(g * head, head), head)
        return (
            pltpu.make_async_copy(key_hbm.at[:, :, cols], keys.at[g], key_sem.at[g]),
            pltpu.make_async_copy(val_hbm.at[:, :, cols], vals.at[g], val_sem.at[g]),
        )

    def load_o(j):
        cols = pl.ds(j * oc, oc) if isinstance(j, int) else pl.ds(pl.multiple_of(j * oc, oc), oc)
        return pltpu.make_async_copy(wo_hbm.at[:, cols], wo.at[j], wo_sem.at[j])

    for g in range(ny):
        for copy in load_cache(g):
            copy.start()
    for j in range(no):
        load_o(j).start()

    def rs(j, d):
        to = lax.rem(x + d, nx)
        rows = pl.ds(pl.multiple_of(to * chunk, chunk), chunk)
        return remote(
            parts.at[j, rows, :], rbuf.at[d - 1, j], rs_s.at[d - 1, j], rs_r.at[d - 1, j], "gx", to
        )

    tokens = xbuf.shape[0] * xbuf.shape[1]
    load_kv().wait()
    for n in range(2):
        parts[nblocks, :, n * head : (n + 1) * head] = jnp.dot(
            xbuf[...].reshape(tokens, xbuf.shape[2]), wkv[n], preferred_element_type=jnp.float32
        )
    for d in range(1, nx):
        rs(nblocks, d).start()

    def block_step(j, carry):
        load_q(j).wait()
        parts[j] = jnp.dot(
            xbuf[...].reshape(tokens, xbuf.shape[2]), wq[j], preferred_element_type=jnp.float32
        )
        for d in range(1, nx):
            rs(j, d).start()
        return carry

    lax.fori_loop(0, nblocks, block_step, 0)

    own = pl.ds(pl.multiple_of(x * chunk, chunk), chunk)
    per_block = bc // head
    heads = nblocks * per_block
    kvbuf[...] = jnp.zeros_like(kvbuf)
    for j in [nblocks] + list(range(nblocks)):
        for d in range(1, nx):
            rs(j, d).wait_recv()
        summed = parts[j, own, :]
        for d in range(1, nx):
            summed = summed + rbuf[d - 1, j]
        for i in range(per_block):
            piece = summed[:, i * head : (i + 1) * head]
            if j < nblocks:
                qbuf[pl.ds(j * per_block + i, chunk, stride=heads), :] = piece
            else:
                kvbuf[pl.ds(i, chunk, stride=4), :] = piece
    local = chunk // ny
    sendbuf[:, : local * heads, :] = (
        qbuf[...].astype(jnp.bfloat16).reshape(ny, local * heads, head)
    )
    sendbuf[:, local * heads :, :] = kvbuf[...].astype(jnp.bfloat16).reshape(ny, local * 4, head)

    def a2a(d):
        to = lax.rem(y + d, ny)
        return remote(sendbuf.at[to], landed.at[y], a_s.at[d - 1], a_r.at[d - 1], "gy", to)

    for d in range(1, ny):
        a2a(d).start()
    landed[y] = sendbuf[y]

    def b2a(d):
        to = lax.rem(y + d, ny)
        return remote(att.at[to], abuf.at[y], b_s.at[d - 1], b_r.at[d - 1], "gy", to)

    def one_head(g, q_block, key, val):
        raw = q_block.astype(jnp.float32)
        swapped = jnp.concatenate([raw[:, head // 2 :], raw[:, : head // 2]], axis=1)
        turned = (raw * cos_ref[...] + swapped * sin_ref[...]).astype(jnp.bfloat16)
        turned_f = turned.astype(jnp.float32)
        slots = key.shape[1]
        group = heads
        count = STEPS * group
        scale = HD ** (-0.5)
        col = lax.broadcasted_iota(jnp.int32, (count, 4 * STEPS), 1)
        step = lax.broadcasted_iota(jnp.int32, (count, 4 * STEPS), 0) // group
        keep_new = (col % 4 == 0) & (col // 4 <= step)
        slot = lax.broadcasted_iota(jnp.int32, (count, slots), 1)
        keys_out, values_out, mixes = [], [], []
        for b in range(key.shape[0]):
            q = turned[b * count : (b + 1) * count]
            base = key.shape[0] * count + b * 4 * STEPS
            kv_turned = turned_f[base : base + 4 * STEPS]
            kv_raw = raw[base : base + 4 * STEPS]
            old = lax.dot_general(
                q, key[b], (((1,), (1,)), ((), ())), preferred_element_type=jnp.float32
            ) * scale
            new = lax.dot_general(
                q, kv_turned.astype(jnp.bfloat16), (((1,), (1,)), ((), ())),
                preferred_element_type=jnp.float32,
            ) * scale
            old = jnp.where(slot < len_ref[b], old, -1e30)
            new = jnp.where(keep_new, new, -1e30)
            highest = jnp.maximum(
                jnp.max(old, axis=-1, keepdims=True), jnp.max(new, axis=-1, keepdims=True)
            )
            old = jnp.exp(old - highest)
            new = jnp.exp(new - highest)
            denom = jnp.sum(old, axis=-1, keepdims=True) + jnp.sum(new, axis=-1, keepdims=True)
            mixed = jnp.dot(old.astype(jnp.bfloat16), val[b], preferred_element_type=jnp.float32)
            new = new.astype(jnp.bfloat16).astype(jnp.float32)
            for r in range(STEPS):
                mixed = mixed + new[:, 4 * r : 4 * r + 1] * kv_raw[4 * r + 1 : 4 * r + 2]
                keys_out.append(kv_turned[4 * r : 4 * r + 1])
                values_out.append(kv_raw[4 * r + 1 : 4 * r + 2])
            mixes.append((mixed / denom).astype(jnp.bfloat16))
        return jnp.concatenate(mixes, axis=0), jnp.concatenate(keys_out + values_out, axis=0)

    def keep(g, mixed, fresh):
        att[g] = mixed
        kv_ref[:, pl.ds(pl.multiple_of(g * head, head), head)] = fresh

    def two_heads(i, carry):
        first = lax.rem(y + 1 + 2 * i, ny)
        second = lax.rem(y + 2 + 2 * i, ny)
        a2a(ny - 1 - 2 * i).wait_recv()

        @pl.when(i < ny // 2 - 1)
        def _():
            a2a(ny - 2 - 2 * i).wait_recv()

        for g in (first, second):
            for copy in load_cache(g):
                copy.wait()
        loaded = [(g, landed[g], keys[g], vals[g]) for g in (first, second)]
        results = [one_head(*items) for items in loaded]
        keep(first, *results[0])
        keep(second, *results[1])
        b2a(2 * i + 1).start()

        @pl.when(i < ny // 2 - 1)
        def _():
            b2a(2 * i + 2).start()

        return carry

    lax.fori_loop(0, ny // 2, two_heads, 0)
    abuf[y] = att[y]
    for d in range(1, ny):
        b2a(d).wait_recv()
    fbuf[...] = abuf[...].astype(jnp.float32).reshape(fbuf.shape)
    for h in range(heads):
        lbuf[x, :, h * head : (h + 1) * head] = fbuf[
            pl.ds(h, chunk, stride=heads), :
        ].astype(jnp.bfloat16)

    def gather(d):
        return remote(
            lbuf.at[x], lbuf.at[x], l_s.at[d - 1], l_r.at[d - 1], "gx", lax.rem(x + d, nx)
        )

    for d in range(1, nx):
        gather(d).start()
    for d in range(1, nx):
        gather(d).wait_recv()

    def pair(j):
        return remote(pbuf.at[j], qland.at[j], c_s.at[j], c_r.at[j], "gy", y + 1 - 2 * c)

    def along(j, d):
        to = lax.rem(z + d, nz)
        return remote(
            zsend.at[j, to], zland.at[d - 1, j], z_s.at[d - 1, j], z_r.at[d - 1, j], "gy", 2 * to + c
        )

    def pass_on(j):
        pair(j).wait_recv()
        chip[j] = prod[j, :, c] + qland[j].astype(jnp.float32)
        zsend[j] = chip[j].astype(jnp.bfloat16)
        for d in range(1, nz):
            along(j, d).start()

    def out_step(j, carry):
        load_o(j).wait()
        prod[j] = jnp.dot(
            lbuf[...].reshape(nx * chunk, lbuf.shape[2]), wo[j], preferred_element_type=jnp.float32
        ).reshape(prod.shape[1:])
        pbuf[j] = prod[j, :, 1 - c].astype(jnp.bfloat16)
        pair(j).start()

        @pl.when(j > 0)
        def _():
            pass_on(j - 1)

        return carry

    lax.fori_loop(0, no, out_step, 0)
    pass_on(no - 1)
    for j in range(no):
        total = chip[j, z]
        for d in range(1, nz):
            along(j, d).wait_recv()
            total = total + zland[d - 1, j].astype(jnp.float32)
        out_ref[:, j * oc : (j + 1) * oc] = total.astype(jnp.bfloat16)

    for d in range(1, ny):
        b2a(d).wait_send()
    for d in range(1, nx):
        gather(d).wait_send()

    def done(j, carry):
        pair(j).wait_send()
        for d in range(1, nz):
            along(j, d).wait_send()
        return carry

    lax.fori_loop(0, no, done, 0)

    for copy in sq_copies:
        copy.wait_send()
    for zz in range(nz):
        block = 2 * zz + c
        hop(block, 2).wait_send()

        @pl.when((zz >= z) & (z > 0))
        def _():
            hop(block, 0).wait_send()

        @pl.when((zz <= z) & (z < nz - 1))
        def _():
            hop(block, 1).wait_send()

    def rs_done(j, carry):
        for d in range(1, nx):
            rs(j, d).wait_send()
        return carry

    lax.fori_loop(0, nblocks + 1, rs_done, 0)
    for d in range(1, ny):
        a2a(d).wait_send()


def with_kernels(
    hidden, norm_gain, w_query, w_keyval, w_out, cache_keys, cache_values, cache_lengths, positions
):
    nx = lax.axis_size("gx")
    ny = lax.axis_size("gy")
    nz = ny // 2
    rows, steps, width = hidden.shape
    mine = rows * steps
    tokens = ny * mine
    chunk = tokens // nx
    local_rows = cache_keys.shape[0]
    local = local_rows * steps
    cols = w_query.shape[1]
    heads = cols // HD
    bc = 256
    nq = cols // bc
    packed = local * heads + local * 4
    vmem = pl.BlockSpec(memory_space=pltpu.VMEM)
    hbm = pl.BlockSpec(memory_space=pl.ANY)
    dma = pltpu.SemaphoreType.DMA
    places = positions.astype(jnp.float32)[:, None] + jnp.arange(steps, dtype=jnp.float32)[None, :]
    angles = places.reshape(local, 1) * rope_rates()[None, :]
    cosine, sine = jnp.cos(angles), jnp.sin(angles)
    cosine = jnp.concatenate([cosine, cosine], axis=-1)
    sine = jnp.concatenate([-sine, sine], axis=-1)
    spread = lambda table: jnp.concatenate(
        [jnp.repeat(table, heads, axis=0), jnp.repeat(table, 4, axis=0)], axis=0
    )
    slots = cache_keys.shape[1]
    oc = 512
    no = w_out.shape[1] // oc
    branch, new = pl.pallas_call(
        functools.partial(layer_kernel, nx, ny),
        out_shape=(
            jax.ShapeDtypeStruct((mine, w_out.shape[1]), jnp.bfloat16),
            jax.ShapeDtypeStruct((2 * local, KVH * HD), jnp.float32),
        ),
        in_specs=[vmem, vmem, pl.BlockSpec(memory_space=pltpu.SMEM), vmem, vmem] + [hbm] * 5,
        out_specs=(vmem, vmem),
        scratch_shapes=[
            pltpu.VMEM((nq, width, bc), jnp.bfloat16),
            pltpu.VMEM(w_keyval.shape, jnp.bfloat16),
            pltpu.VMEM((ny, mine, width), jnp.bfloat16),
            pltpu.VMEM((nx, mine, 128), jnp.float32),
            pltpu.VMEM((nq + 1, tokens, bc), jnp.float32),
            pltpu.VMEM((nx - 1, nq + 1, chunk, bc), jnp.float32),
            pltpu.VMEM((chunk * heads, HD), jnp.float32),
            pltpu.VMEM((chunk * 4, HD), jnp.float32),
            pltpu.VMEM((ny, packed, HD), jnp.bfloat16),
            pltpu.VMEM((ny, packed, HD), jnp.bfloat16),
            pltpu.VMEM((ny, local_rows, slots, HD), jnp.bfloat16),
            pltpu.VMEM((ny, local_rows, slots, HD), jnp.bfloat16),
            pltpu.VMEM((no, cols, oc), jnp.bfloat16),
            pltpu.VMEM((ny, local * heads, HD), jnp.bfloat16),
            pltpu.VMEM((ny, local * heads, HD), jnp.bfloat16),
            pltpu.VMEM((chunk * heads, HD), jnp.float32),
            pltpu.VMEM((nx, chunk, cols), jnp.bfloat16),
            pltpu.VMEM((no, nz, 2, mine, oc), jnp.float32),
            pltpu.VMEM((no, nz, mine, oc), jnp.bfloat16),
            pltpu.VMEM((no, nz, mine, oc), jnp.bfloat16),
            pltpu.VMEM((no, nz, mine, oc), jnp.float32),
            pltpu.VMEM((no, nz, mine, oc), jnp.bfloat16),
            pltpu.VMEM((nz - 1, no, mine, oc), jnp.bfloat16),
            dma((nq,)),
            dma(()),
            dma((nx - 1,)),
            dma((nx - 1,)),
            dma((ny, 3)),
            dma((ny,)),
            dma((nx - 1, nq + 1)),
            dma((nx - 1, nq + 1)),
            dma((ny - 1,)),
            dma((ny - 1,)),
            dma((ny,)),
            dma((ny,)),
            dma((no,)),
            dma((ny - 1,)),
            dma((ny - 1,)),
            dma((nx - 1,)),
            dma((nx - 1,)),
            dma((no,)),
            dma((no,)),
            dma((nz - 1, no)),
            dma((nz - 1, no)),
        ],
        compiler_params=pltpu.CompilerParams(
            collective_id=0, has_side_effects=True, vmem_limit_bytes=60 * 1024 * 1024
        ),
        name="layer",
    )(
        hidden.reshape(mine, width), norm_gain.reshape(1, width), cache_lengths,
        spread(cosine), spread(sine), w_query, w_keyval, cache_keys, cache_values, w_out,
    )
    new_keyvals = new.astype(jnp.bfloat16).reshape(2, local_rows, steps, KVH * HD)
    return (branch.reshape(rows, steps, -1), new_keyvals)


def on_device(*args):
    hidden, _, w_query, w_keyval, w_out, cache_keys = args[:6]
    nx, ny = lax.axis_size("gx"), lax.axis_size("gy")
    local = cache_keys.shape[0] * hidden.shape[1]
    fits = (
        w_keyval.shape[2] == HD
        and ny == KVH
        and hidden.shape[1] == STEPS
        and hidden.shape[0] * hidden.shape[1] % 16 == 0
        and local == 4
        and w_query.shape[1] % 256 == 0
        and w_out.shape[1] % 512 == 0
        and nx > 1
    )
    return with_kernels(*args) if fits else plain(*args)


def solution(mesh):
    return jax.shard_map(
        on_device,
        mesh=mesh,
        in_specs=(
            P("gy", None, "gx"),
            P("gx"),
            P("gx", "gy"),
            P(None, "gx", "gy"),
            P("gy", "gx"),
            P(("gx", "gy"), None, None),
            P(("gx", "gy"), None, None),
            P(("gx", "gy")),
            P(("gx", "gy")),
        ),
        out_specs=(P("gy", None, "gx"), P(None, ("gx", "gy"), None, None)),
        check_vma=False,
    )
```

```python
import functools
import math

import jax
import jax.numpy as jnp
from jax import lax
from jax.experimental import pallas as pl
from jax.experimental.pallas import tpu as pltpu
from jax.sharding import PartitionSpec as P

D = 16384
HQ = 128
KVH = 8
HD = 128
STEPS = 2


norm_epsilon = 1e-05


def rope_rates():
    index = jnp.arange(HD // 2, dtype=jnp.float32)
    rates = 1.0 / jnp.power(500000.0, 2.0 * index / HD)
    wavelength = 2.0 * math.pi / rates
    smooth = (8192.0 / wavelength - 1.0) / 3.0
    blended = (1.0 - smooth) * rates / 8.0 + smooth * rates
    return jnp.where(
        wavelength > 8192.0, rates / 8.0, jnp.where(wavelength < 2048.0, rates, blended)
    )


def rotate(vectors, places):
    angles = places[..., None, None] * rope_rates()
    half_size = vectors.shape[-1] // 2
    first_half = vectors[..., :half_size]
    second_half = vectors[..., half_size:]
    cosine = jnp.cos(angles)
    sine = jnp.sin(angles)
    return jnp.concatenate(
        [first_half * cosine - second_half * sine, second_half * cosine + first_half * sine],
        axis=-1,
    )


def attend(queries, fresh_keys, fresh_values, cached_keys, cached_values, lengths):
    rows, steps = (queries.shape[0], queries.shape[1])
    slots = cached_keys.shape[1]
    grouped = queries.reshape(rows, steps, KVH, HQ // KVH, HD)
    old_keys = cached_keys.reshape(rows, slots, KVH, HD)
    old_values = cached_values.reshape(rows, slots, KVH, HD)
    score_scale = HD ** (-0.5)
    cached = (
        jnp.einsum("bskgd,btkd->bskgt", grouped, old_keys, preferred_element_type=jnp.float32)
        * score_scale
    )
    fresh = (
        jnp.einsum("bskgd,brkd->bskgr", grouped, fresh_keys, preferred_element_type=jnp.float32)
        * score_scale
    )
    slot_valid = jnp.arange(slots)[None, :] < lengths[:, None]
    step_valid = jnp.arange(steps)[None, :] <= jnp.arange(steps)[:, None]
    cached = jnp.where(slot_valid[:, None, None, None, :], cached, -1e30)
    fresh = jnp.where(step_valid[None, :, None, None, :], fresh, -1e30)
    highest = jnp.maximum(jnp.max(cached, axis=-1), jnp.max(fresh, axis=-1))[..., None]
    weights_old = jnp.exp(cached - highest)
    weights_new = jnp.exp(fresh - highest)
    denom = jnp.sum(weights_old, axis=-1) + jnp.sum(weights_new, axis=-1)
    mixed = jnp.einsum(
        "bskgt,btkd->bskgd",
        weights_old.astype(jnp.bfloat16),
        old_values,
        preferred_element_type=jnp.float32,
    )
    mixed = mixed + jnp.einsum(
        "bskgr,brkd->bskgd",
        weights_new.astype(jnp.bfloat16),
        fresh_values,
        preferred_element_type=jnp.float32,
    )
    return (mixed / denom[..., None]).astype(jnp.bfloat16).reshape(rows, steps, HQ * HD)


def plain(
    hidden, norm_gain, w_query, w_keyval, w_out, cache_keys, cache_values, cache_lengths, positions
):
    steps = hidden.shape[1]
    features = hidden.astype(jnp.float32)
    squares = jnp.sum(features * features, axis=-1)
    square_sums = lax.psum(squares, "gx")
    inverse = lax.rsqrt(square_sums / D + norm_epsilon)
    normed = (features * inverse[..., None] * norm_gain.astype(jnp.float32)).astype(jnp.bfloat16)
    shard_rows = lax.all_gather(normed, "gy", axis=0, tiled=True)
    flattened = shard_rows.reshape(-1, shard_rows.shape[2])
    products = [
        jnp.dot(flattened, w_query, preferred_element_type=jnp.float32),
        jnp.dot(flattened, w_keyval[0], preferred_element_type=jnp.float32),
        jnp.dot(flattened, w_keyval[1], preferred_element_type=jnp.float32),
    ]
    partial_sums = jnp.concatenate(products, axis=-1).reshape(shard_rows.shape[0], steps, -1)
    width_parts = lax.axis_size("gx")
    head_parts = lax.axis_size("gy")
    block_rows = partial_sums.shape[0] // width_parts
    summed = lax.psum(partial_sums, "gx")
    summed = lax.dynamic_slice_in_dim(summed, lax.axis_index("gx") * block_rows, block_rows, 0)
    own_rows = summed.astype(jnp.bfloat16)
    arrived = lax.all_to_all(own_rows, "gy", split_axis=0, concat_axis=2, tiled=True)
    local_rows = arrived.shape[0]
    pieces = arrived.reshape(local_rows, steps, head_parts, -1)
    query_cols = w_query.shape[1]
    keyval_cols = w_keyval.shape[2]
    queries = pieces[..., :query_cols].reshape(local_rows, steps, HQ, HD)
    fresh_keys = pieces[..., query_cols : query_cols + keyval_cols].reshape(
        local_rows, steps, KVH, HD
    )
    fresh_values = pieces[..., query_cols + keyval_cols :].reshape(local_rows, steps, KVH, HD)
    places = positions.astype(jnp.float32)[:, None] + jnp.arange(steps, dtype=jnp.float32)[None, :]
    turned_queries = rotate(queries.astype(jnp.float32), places).astype(jnp.bfloat16)
    turned_keys = rotate(fresh_keys.astype(jnp.float32), places).astype(jnp.bfloat16)
    new_keyvals = jnp.stack(
        [
            turned_keys.reshape(local_rows, steps, KVH * HD),
            fresh_values.reshape(local_rows, steps, KVH * HD),
        ]
    )
    attended = attend(
        turned_queries, turned_keys, fresh_values, cache_keys, cache_values, cache_lengths
    )
    returned = lax.all_to_all(attended, "gy", split_axis=2, concat_axis=0, tiled=True)
    rows_all = lax.all_gather(returned, "gx", axis=0, tiled=True)
    head_cols = rows_all.shape[2]
    all_rows = rows_all.shape[0]
    out_rows_here = all_rows // head_parts
    product = jnp.dot(
        rows_all.reshape(lax.axis_size("gy") * out_rows_here * steps, head_cols),
        w_out,
        preferred_element_type=jnp.float32,
    )
    branch = lax.psum_scatter(
        product.reshape(lax.axis_size("gy") * out_rows_here, steps, -1),
        "gy",
        scatter_dimension=0,
        tiled=True,
    )
    return (branch.astype(jnp.bfloat16), new_keyvals)


def peer_id(axis, index):
    return {axis: index}


def remote(src, dst, send_sem, recv_sem, axis, index):
    return pltpu.make_async_remote_copy(
        src_ref=src,
        dst_ref=dst,
        send_sem=send_sem,
        recv_sem=recv_sem,
        device_id=peer_id(axis, index),
        device_id_type=pl.DeviceIdType.MESH,
    )


def greet(x, y, nx, ny):
    barrier = pltpu.get_barrier_semaphore()
    for d in range(1, nx):
        pl.semaphore_signal(
            barrier, inc=1, device_id=peer_id("gx", lax.rem(x + d, nx)),
            device_id_type=pl.DeviceIdType.MESH,
        )
    for d in range(1, ny):
        pl.semaphore_signal(
            barrier, inc=1, device_id=peer_id("gy", lax.rem(y + d, ny)),
            device_id_type=pl.DeviceIdType.MESH,
        )
    pl.semaphore_wait(barrier, nx - 1 + ny - 1)


def layer_kernel(
    nx, ny, x_ref, gain_ref, len_ref, cos_ref, sin_ref, wq_hbm, wkv_hbm, key_hbm, val_hbm, wo_hbm,
    out_ref, kv_ref,
    xf, cosbuf, sinbuf, wq, wkv, xbuf, sqbuf, parts, rbuf, qbuf, kvbuf, sendbuf, landed,
    keys, vals, wo, att, abuf, fbuf, lbuf, prod, pbuf, qland, chip, zsend, zland,
    wq_sem, wkv_sem, sq_s, sq_r, g_s, g_r, rs_s, rs_r, a_s, a_r,
    key_sem, val_sem, wo_sem, b_s, b_r, l_s, l_r, c_s, c_r, z_s, z_r,
):
    x = lax.axis_index("gx")
    y = lax.axis_index("gy")
    nz = ny // 2
    z = y // 2
    c = lax.rem(y, 2)
    nblocks = wq.shape[0]
    bc = wq.shape[2]
    head = wkv.shape[2]
    chunk = rbuf.shape[2]
    no = wo.shape[0]
    oc = wo.shape[2]

    def load_q(j):
        cols = pl.ds(j * bc, bc) if isinstance(j, int) else pl.ds(pl.multiple_of(j * bc, bc), bc)
        return pltpu.make_async_copy(wq_hbm.at[:, cols], wq.at[j], wq_sem.at[j])

    def load_kv():
        return pltpu.make_async_copy(wkv_hbm, wkv, wkv_sem)

    load_kv().start()
    for j in range(nblocks):
        load_q(j).start()

    count = x_ref.shape[1]
    for i in range(x_ref.shape[0]):
        xf[count * i : count * (i + 1), :] = x_ref[i].astype(jnp.float32)
    features = xf[...]
    squares = jnp.sum(features * features, axis=-1, keepdims=True)
    sqbuf[0] = jnp.broadcast_to(squares, sqbuf.shape[1:])
    greet(x, y, nx, ny)
    sq_copies = [
        remote(sqbuf.at[0], sqbuf.at[d], sq_s.at[d - 1], sq_r.at[d - 1], "gx", lax.rem(x + d, nx))
        for d in range(1, nx)
    ]
    for copy in sq_copies:
        copy.start()
    for copy in sq_copies:
        copy.wait_recv()
    total = sqbuf[0]
    for d in range(1, nx):
        total = total + sqbuf[d]
    inverse = lax.rsqrt(total[:, :1] / D + norm_epsilon)
    normed = (
        features * inverse * gain_ref[...].astype(jnp.float32).reshape(1, features.shape[1])
    ).astype(jnp.bfloat16)
    half = xbuf.shape[3]
    for t in range(2):
        xbuf[t, y] = normed[:, t * half : (t + 1) * half]

    def hop(t, block, k):
        dest = (y - 2, y + 2, y + 1 - 2 * c)[k]
        return remote(
            xbuf.at[t, block], xbuf.at[t, block], g_s.at[t, block, k], g_r.at[t, block], "gy", dest
        )

    def begin(t):
        @pl.when(z > 0)
        def _():
            hop(t, y, 0).start()

        @pl.when(z < nz - 1)
        def _():
            hop(t, y, 1).start()

        hop(t, y, 2).start()

    def forward(t, d):
        @pl.when(z - d >= 0)
        def _():
            block = y - 2 * d
            hop(t, block, 2).wait_recv()

            @pl.when(z < nz - 1)
            def _():
                hop(t, block, 1).start()

            hop(t, block, 2).start()

        @pl.when(z + d < nz)
        def _():
            block = y + 2 * d
            hop(t, block, 2).wait_recv()

            @pl.when(z > 0)
            def _():
                hop(t, block, 0).start()

            hop(t, block, 2).start()

    def from_pair(t):
        for zz in range(nz):
            hop(t, 2 * zz + 1 - c, 2).wait_recv()

    begin(0)
    for d in range(1, nz):
        forward(0, d)
        if d == 1:
            begin(1)
    from_pair(0)

    def load_cache(g):
        cols = pl.ds(g * head, head) if isinstance(g, int) else pl.ds(pl.multiple_of(g * head, head), head)
        return (
            pltpu.make_async_copy(key_hbm.at[:, :, cols], keys.at[g], key_sem.at[g]),
            pltpu.make_async_copy(val_hbm.at[:, :, cols], vals.at[g], val_sem.at[g]),
        )

    def load_o(j):
        cols = pl.ds(j * oc, oc) if isinstance(j, int) else pl.ds(pl.multiple_of(j * oc, oc), oc)
        return pltpu.make_async_copy(wo_hbm.at[:, cols], wo.at[j], wo_sem.at[j])

    for g in range(ny):
        for copy in load_cache(g):
            copy.start()
    for j in range(no):
        load_o(j).start()

    def rs(j, d):
        to = lax.rem(x + d, nx)
        rows = pl.ds(pl.multiple_of(to * chunk, chunk), chunk)
        return remote(
            parts.at[j, rows, :], rbuf.at[d - 1, j], rs_s.at[d - 1, j], rs_r.at[d - 1, j], "gx", to
        )

    tokens = xbuf.shape[1] * xbuf.shape[2]

    def times(t, weights):
        return jnp.dot(
            xbuf[t].reshape(tokens, half), weights, preferred_element_type=jnp.float32
        )

    def first_half(j, carry):
        load_q(j).wait()
        parts[j] = times(0, wq[j, :half])
        return carry

    load_kv().wait()
    for n in range(2):
        parts[nblocks, :, n * head : (n + 1) * head] = times(0, wkv[n, :half])
    done = 0
    for d in range(1, nz):
        upto = nblocks * d // nz
        lax.fori_loop(done, upto, first_half, 0)
        forward(1, d)
        done = upto
    lax.fori_loop(done, nblocks, first_half, 0)
    from_pair(1)
    for n in range(2):
        parts[nblocks, :, n * head : (n + 1) * head] += times(1, wkv[n, half:])
    for d in range(1, nx):
        rs(nblocks, d).start()

    def second_half(j, carry):
        parts[j] += times(1, wq[j, half:])
        for d in range(1, nx):
            rs(j, d).start()
        return carry

    lax.fori_loop(0, nblocks, second_half, 0)

    own = pl.ds(pl.multiple_of(x * chunk, chunk), chunk)
    per_block = bc // head
    heads = nblocks * per_block
    kvbuf[...] = jnp.zeros_like(kvbuf)
    for j in [nblocks] + list(range(nblocks)):
        for d in range(1, nx):
            rs(j, d).wait_recv()
        summed = parts[j, own, :]
        for d in range(1, nx):
            summed = summed + rbuf[d - 1, j]
        for i in range(per_block):
            piece = summed[:, i * head : (i + 1) * head]
            if j < nblocks:
                qbuf[pl.ds(j * per_block + i, chunk, stride=heads), :] = piece
            else:
                kvbuf[pl.ds(i, chunk, stride=4), :] = piece
    local = chunk // ny
    sendbuf[:, : local * heads, :] = (
        qbuf[...].astype(jnp.bfloat16).reshape(ny, local * heads, head)
    )
    sendbuf[:, local * heads :, :] = kvbuf[...].astype(jnp.bfloat16).reshape(ny, local * 4, head)

    def a2a(d):
        to = lax.rem(y + d, ny)
        return remote(sendbuf.at[to], landed.at[y], a_s.at[d - 1], a_r.at[d - 1], "gy", to)

    for d in range(1, ny):
        a2a(d).start()
    landed[y] = sendbuf[y]

    for buf, first, last in ((cosbuf, 1.0, 1.0), (sinbuf, -1.0, 1.0)):
        table = cos_ref if buf is cosbuf else sin_ref
        lines = []
        for b in range(table.shape[0]):
            line = table[b]
            line = jnp.concatenate([line * first, line * last], axis=1)
            lines += [line[r : r + 1] for r in range(STEPS)]
        for r, line in enumerate(lines):
            buf[r * heads : (r + 1) * heads, :] = jnp.broadcast_to(line, (heads, head))
        tail = [jnp.broadcast_to(line, (4, head)) for line in lines]
        buf[local * heads :, :] = jnp.concatenate(tail, axis=0)

    def b2a(d):
        to = lax.rem(y + d, ny)
        return remote(att.at[to], abuf.at[y], b_s.at[d - 1], b_r.at[d - 1], "gy", to)

    def one_head(g, q_block, key, val):
        raw = q_block.astype(jnp.float32)
        swapped = jnp.concatenate([raw[:, head // 2 :], raw[:, : head // 2]], axis=1)
        turned = (raw * cosbuf[...] + swapped * sinbuf[...]).astype(jnp.bfloat16)
        turned_f = turned.astype(jnp.float32)
        slots = key.shape[1]
        group = heads
        count = STEPS * group
        scale = HD ** (-0.5)
        col = lax.broadcasted_iota(jnp.int32, (count, 4 * STEPS), 1)
        step = lax.broadcasted_iota(jnp.int32, (count, 4 * STEPS), 0) // group
        keep_new = (col % 4 == 0) & (col // 4 <= step)
        slot = lax.broadcasted_iota(jnp.int32, (count, slots), 1)
        keys_out, values_out, mixes = [], [], []
        for b in range(key.shape[0]):
            q = turned[b * count : (b + 1) * count]
            base = key.shape[0] * count + b * 4 * STEPS
            kv_turned = turned_f[base : base + 4 * STEPS]
            kv_raw = raw[base : base + 4 * STEPS]
            old = lax.dot_general(
                q, key[b], (((1,), (1,)), ((), ())), preferred_element_type=jnp.float32
            ) * scale
            new = lax.dot_general(
                q, kv_turned.astype(jnp.bfloat16), (((1,), (1,)), ((), ())),
                preferred_element_type=jnp.float32,
            ) * scale
            old = jnp.where(slot < len_ref[b], old, -1e30)
            new = jnp.where(keep_new, new, -1e30)
            highest = jnp.maximum(
                jnp.max(old, axis=-1, keepdims=True), jnp.max(new, axis=-1, keepdims=True)
            )
            old = jnp.exp(old - highest)
            new = jnp.exp(new - highest)
            denom = jnp.sum(old, axis=-1, keepdims=True) + jnp.sum(new, axis=-1, keepdims=True)
            mixed = jnp.dot(old.astype(jnp.bfloat16), val[b], preferred_element_type=jnp.float32)
            new = new.astype(jnp.bfloat16).astype(jnp.float32)
            for r in range(STEPS):
                mixed = mixed + new[:, 4 * r : 4 * r + 1] * kv_raw[4 * r + 1 : 4 * r + 2]
            for out, block, at in ((keys_out, kv_turned, 0), (values_out, kv_raw, 1)):
                lines = [block[4 * r + at : 4 * r + at + 1] for r in range(STEPS)]
                out.append(jnp.concatenate(lines, axis=0).astype(jnp.bfloat16))
            mixes.append((mixed / denom).astype(jnp.bfloat16))
        return jnp.concatenate(mixes, axis=0), (keys_out, values_out)

    def keep(g, mixed, fresh):
        att[g] = mixed
        for n in range(2):
            for b in range(kv_ref.shape[1]):
                kv_ref[n, b, :, pl.ds(pl.multiple_of(g * head, head), head)] = fresh[n][b]

    def two_heads(i, carry):
        first = lax.rem(y + 1 + 2 * i, ny)
        second = lax.rem(y + 2 + 2 * i, ny)
        a2a(ny - 1 - 2 * i).wait_recv()

        @pl.when(i < ny // 2 - 1)
        def _():
            a2a(ny - 2 - 2 * i).wait_recv()

        for g in (first, second):
            for copy in load_cache(g):
                copy.wait()
        loaded = [(g, landed[g], keys[g], vals[g]) for g in (first, second)]
        results = [one_head(*items) for items in loaded]
        keep(first, *results[0])
        keep(second, *results[1])
        b2a(2 * i + 1).start()

        @pl.when(i < ny // 2 - 1)
        def _():
            b2a(2 * i + 2).start()

        return carry

    lax.fori_loop(0, ny // 2, two_heads, 0)
    abuf[y] = att[y]
    for d in range(1, ny):
        b2a(d).wait_recv()
    fbuf[...] = abuf[...].astype(jnp.float32).reshape(fbuf.shape)

    def gather(t, d):
        return remote(
            lbuf.at[t, x], lbuf.at[t, x], l_s.at[t, d - 1], l_r.at[t, d - 1], "gx", lax.rem(x + d, nx)
        )

    kept = heads // 2
    for t in range(2):
        for h in range(kept):
            lbuf[t, x, :, h * head : (h + 1) * head] = fbuf[
                pl.ds(t * kept + h, chunk, stride=heads), :
            ].astype(jnp.bfloat16)
        for d in range(1, nx):
            gather(t, d).start()

    def out_times(t, j):
        depth = kept * head
        return jnp.dot(
            lbuf[t].reshape(nx * chunk, depth), wo[j, t * depth : (t + 1) * depth],
            preferred_element_type=jnp.float32,
        ).reshape(prod.shape[1:])

    for d in range(1, nx):
        gather(0, d).wait_recv()

    def out_first(j, carry):
        load_o(j).wait()
        prod[j] = out_times(0, j)
        return carry

    lax.fori_loop(0, no, out_first, 0)
    for d in range(1, nx):
        gather(1, d).wait_recv()

    def pair(j):
        return remote(pbuf.at[j], qland.at[j], c_s.at[j], c_r.at[j], "gy", y + 1 - 2 * c)

    def along(j, d):
        to = lax.rem(z + d, nz)
        return remote(
            zsend.at[j, to], zland.at[d - 1, j], z_s.at[d - 1, j], z_r.at[d - 1, j], "gy", 2 * to + c
        )

    def pass_on(j):
        pair(j).wait_recv()
        chip[j] = prod[j, :, c] + qland[j].astype(jnp.float32)
        zsend[j] = chip[j].astype(jnp.bfloat16)
        for d in range(1, nz):
            along(j, d).start()

    def out_step(j, carry):
        prod[j] += out_times(1, j)
        pbuf[j] = prod[j, :, 1 - c].astype(jnp.bfloat16)
        pair(j).start()

        @pl.when(j > 0)
        def _():
            pass_on(j - 1)

        return carry

    lax.fori_loop(0, no, out_step, 0)
    pass_on(no - 1)
    for j in range(no):
        total = chip[j, z]
        for d in range(1, nz):
            along(j, d).wait_recv()
            total = total + zland[d - 1, j].astype(jnp.float32)
        for i in range(out_ref.shape[0]):
            out_ref[i, :, j * oc : (j + 1) * oc] = total[count * i : count * (i + 1)].astype(
                jnp.bfloat16
            )

    for d in range(1, ny):
        b2a(d).wait_send()
    for t in range(2):
        for d in range(1, nx):
            gather(t, d).wait_send()

    def done(j, carry):
        pair(j).wait_send()
        for d in range(1, nz):
            along(j, d).wait_send()
        return carry

    lax.fori_loop(0, no, done, 0)

    for copy in sq_copies:
        copy.wait_send()
    for t in range(2):
        for zz in range(nz):
            block = 2 * zz + c
            hop(t, block, 2).wait_send()

            @pl.when((zz >= z) & (z > 0))
            def _():
                hop(t, block, 0).wait_send()

            @pl.when((zz <= z) & (z < nz - 1))
            def _():
                hop(t, block, 1).wait_send()

    def rs_done(j, carry):
        for d in range(1, nx):
            rs(j, d).wait_send()
        return carry

    lax.fori_loop(0, nblocks + 1, rs_done, 0)
    for d in range(1, ny):
        a2a(d).wait_send()


def with_kernels(
    hidden, norm_gain, w_query, w_keyval, w_out, cache_keys, cache_values, cache_lengths, positions
):
    nx = lax.axis_size("gx")
    ny = lax.axis_size("gy")
    nz = ny // 2
    rows, steps, width = hidden.shape
    mine = rows * steps
    tokens = ny * mine
    chunk = tokens // nx
    local_rows = cache_keys.shape[0]
    local = local_rows * steps
    cols = w_query.shape[1]
    heads = cols // HD
    bc = 256
    nq = cols // bc
    packed = local * heads + local * 4
    vmem = pl.BlockSpec(memory_space=pltpu.VMEM)
    hbm = pl.BlockSpec(memory_space=pl.ANY)
    dma = pltpu.SemaphoreType.DMA
    places = positions.astype(jnp.float32)[:, None] + jnp.arange(steps, dtype=jnp.float32)[None, :]
    angles = places[..., None] * rope_rates()
    slots = cache_keys.shape[1]
    oc = 512
    no = w_out.shape[1] // oc
    return pl.pallas_call(
        functools.partial(layer_kernel, nx, ny),
        out_shape=(
            jax.ShapeDtypeStruct((rows, steps, w_out.shape[1]), jnp.bfloat16),
            jax.ShapeDtypeStruct((2, local_rows, steps, KVH * HD), jnp.bfloat16),
        ),
        in_specs=[vmem, vmem, pl.BlockSpec(memory_space=pltpu.SMEM), vmem, vmem] + [hbm] * 5,
        out_specs=(vmem, vmem),
        scratch_shapes=[
            pltpu.VMEM((mine, width), jnp.float32),
            pltpu.VMEM((packed, HD), jnp.float32),
            pltpu.VMEM((packed, HD), jnp.float32),
            pltpu.VMEM((nq, width, bc), jnp.bfloat16),
            pltpu.VMEM(w_keyval.shape, jnp.bfloat16),
            pltpu.VMEM((2, ny, mine, width // 2), jnp.bfloat16),
            pltpu.VMEM((nx, mine, 128), jnp.float32),
            pltpu.VMEM((nq + 1, tokens, bc), jnp.float32),
            pltpu.VMEM((nx - 1, nq + 1, chunk, bc), jnp.float32),
            pltpu.VMEM((chunk * heads, HD), jnp.float32),
            pltpu.VMEM((chunk * 4, HD), jnp.float32),
            pltpu.VMEM((ny, packed, HD), jnp.bfloat16),
            pltpu.VMEM((ny, packed, HD), jnp.bfloat16),
            pltpu.VMEM((ny, local_rows, slots, HD), jnp.bfloat16),
            pltpu.VMEM((ny, local_rows, slots, HD), jnp.bfloat16),
            pltpu.VMEM((no, cols, oc), jnp.bfloat16),
            pltpu.VMEM((ny, local * heads, HD), jnp.bfloat16),
            pltpu.VMEM((ny, local * heads, HD), jnp.bfloat16),
            pltpu.VMEM((chunk * heads, HD), jnp.float32),
            pltpu.VMEM((2, nx, chunk, cols // 2), jnp.bfloat16),
            pltpu.VMEM((no, nz, 2, mine, oc), jnp.float32),
            pltpu.VMEM((no, nz, mine, oc), jnp.bfloat16),
            pltpu.VMEM((no, nz, mine, oc), jnp.bfloat16),
            pltpu.VMEM((no, nz, mine, oc), jnp.float32),
            pltpu.VMEM((no, nz, mine, oc), jnp.bfloat16),
            pltpu.VMEM((nz - 1, no, mine, oc), jnp.bfloat16),
            dma((nq,)),
            dma(()),
            dma((nx - 1,)),
            dma((nx - 1,)),
            dma((2, ny, 3)),
            dma((2, ny)),
            dma((nx - 1, nq + 1)),
            dma((nx - 1, nq + 1)),
            dma((ny - 1,)),
            dma((ny - 1,)),
            dma((ny,)),
            dma((ny,)),
            dma((no,)),
            dma((ny - 1,)),
            dma((ny - 1,)),
            dma((2, nx - 1)),
            dma((2, nx - 1)),
            dma((no,)),
            dma((no,)),
            dma((nz - 1, no)),
            dma((nz - 1, no)),
        ],
        compiler_params=pltpu.CompilerParams(
            collective_id=0, has_side_effects=True, vmem_limit_bytes=60 * 1024 * 1024
        ),
        name="layer",
    )(
        hidden, norm_gain, cache_lengths, jnp.cos(angles), jnp.sin(angles),
        w_query, w_keyval, cache_keys, cache_values, w_out,
    )


def on_device(*args):
    hidden, _, w_query, w_keyval, w_out, cache_keys = args[:6]
    nx, ny = lax.axis_size("gx"), lax.axis_size("gy")
    local = cache_keys.shape[0] * hidden.shape[1]
    fits = (
        w_keyval.shape[2] == HD
        and ny == KVH
        and hidden.shape[1] == STEPS
        and hidden.shape[0] * hidden.shape[1] % 16 == 0
        and local == 4
        and w_query.shape[1] % 256 == 0
        and w_out.shape[1] % 512 == 0
        and nx > 1
    )
    return with_kernels(*args) if fits else plain(*args)


def solution(mesh):
    return jax.shard_map(
        on_device,
        mesh=mesh,
        in_specs=(
            P("gy", None, "gx"),
            P("gx"),
            P("gx", "gy"),
            P(None, "gx", "gy"),
            P("gy", "gx"),
            P(("gx", "gy"), None, None),
            P(("gx", "gy"), None, None),
            P(("gx", "gy")),
            P(("gx", "gy")),
        ),
        out_specs=(P("gy", None, "gx"), P(None, ("gx", "gy"), None, None)),
        check_vma=False,
    )
```

```python
import functools
import math

import jax
import jax.numpy as jnp
from jax import lax
from jax.experimental import pallas as pl
from jax.experimental.pallas import tpu as pltpu
from jax.sharding import PartitionSpec as P

D = 16384
HQ = 128
KVH = 8
HD = 128
STEPS = 2


norm_epsilon = 1e-05


def rope_rates():
    index = jnp.arange(HD // 2, dtype=jnp.float32)
    rates = 1.0 / jnp.power(500000.0, 2.0 * index / HD)
    wavelength = 2.0 * math.pi / rates
    smooth = (8192.0 / wavelength - 1.0) / 3.0
    blended = (1.0 - smooth) * rates / 8.0 + smooth * rates
    return jnp.where(
        wavelength > 8192.0, rates / 8.0, jnp.where(wavelength < 2048.0, rates, blended)
    )


def rotate(vectors, places):
    angles = places[..., None, None] * rope_rates()
    half_size = vectors.shape[-1] // 2
    first_half = vectors[..., :half_size]
    second_half = vectors[..., half_size:]
    cosine = jnp.cos(angles)
    sine = jnp.sin(angles)
    return jnp.concatenate(
        [first_half * cosine - second_half * sine, second_half * cosine + first_half * sine],
        axis=-1,
    )


def attend(queries, fresh_keys, fresh_values, cached_keys, cached_values, lengths):
    rows, steps = (queries.shape[0], queries.shape[1])
    slots = cached_keys.shape[1]
    grouped = queries.reshape(rows, steps, KVH, HQ // KVH, HD)
    old_keys = cached_keys.reshape(rows, slots, KVH, HD)
    old_values = cached_values.reshape(rows, slots, KVH, HD)
    score_scale = HD ** (-0.5)
    cached = (
        jnp.einsum("bskgd,btkd->bskgt", grouped, old_keys, preferred_element_type=jnp.float32)
        * score_scale
    )
    fresh = (
        jnp.einsum("bskgd,brkd->bskgr", grouped, fresh_keys, preferred_element_type=jnp.float32)
        * score_scale
    )
    slot_valid = jnp.arange(slots)[None, :] < lengths[:, None]
    step_valid = jnp.arange(steps)[None, :] <= jnp.arange(steps)[:, None]
    cached = jnp.where(slot_valid[:, None, None, None, :], cached, -1e30)
    fresh = jnp.where(step_valid[None, :, None, None, :], fresh, -1e30)
    highest = jnp.maximum(jnp.max(cached, axis=-1), jnp.max(fresh, axis=-1))[..., None]
    weights_old = jnp.exp(cached - highest)
    weights_new = jnp.exp(fresh - highest)
    denom = jnp.sum(weights_old, axis=-1) + jnp.sum(weights_new, axis=-1)
    mixed = jnp.einsum(
        "bskgt,btkd->bskgd",
        weights_old.astype(jnp.bfloat16),
        old_values,
        preferred_element_type=jnp.float32,
    )
    mixed = mixed + jnp.einsum(
        "bskgr,brkd->bskgd",
        weights_new.astype(jnp.bfloat16),
        fresh_values,
        preferred_element_type=jnp.float32,
    )
    return (mixed / denom[..., None]).astype(jnp.bfloat16).reshape(rows, steps, HQ * HD)


def plain(
    hidden, norm_gain, w_query, w_keyval, w_out, cache_keys, cache_values, cache_lengths, positions
):
    steps = hidden.shape[1]
    features = hidden.astype(jnp.float32)
    squares = jnp.sum(features * features, axis=-1)
    square_sums = lax.psum(squares, "gx")
    inverse = lax.rsqrt(square_sums / D + norm_epsilon)
    normed = (features * inverse[..., None] * norm_gain.astype(jnp.float32)).astype(jnp.bfloat16)
    shard_rows = lax.all_gather(normed, "gy", axis=0, tiled=True)
    flattened = shard_rows.reshape(-1, shard_rows.shape[2])
    products = [
        jnp.dot(flattened, w_query, preferred_element_type=jnp.float32),
        jnp.dot(flattened, w_keyval[0], preferred_element_type=jnp.float32),
        jnp.dot(flattened, w_keyval[1], preferred_element_type=jnp.float32),
    ]
    partial_sums = jnp.concatenate(products, axis=-1).reshape(shard_rows.shape[0], steps, -1)
    width_parts = lax.axis_size("gx")
    head_parts = lax.axis_size("gy")
    block_rows = partial_sums.shape[0] // width_parts
    summed = lax.psum(partial_sums, "gx")
    summed = lax.dynamic_slice_in_dim(summed, lax.axis_index("gx") * block_rows, block_rows, 0)
    own_rows = summed.astype(jnp.bfloat16)
    arrived = lax.all_to_all(own_rows, "gy", split_axis=0, concat_axis=2, tiled=True)
    local_rows = arrived.shape[0]
    pieces = arrived.reshape(local_rows, steps, head_parts, -1)
    query_cols = w_query.shape[1]
    keyval_cols = w_keyval.shape[2]
    queries = pieces[..., :query_cols].reshape(local_rows, steps, HQ, HD)
    fresh_keys = pieces[..., query_cols : query_cols + keyval_cols].reshape(
        local_rows, steps, KVH, HD
    )
    fresh_values = pieces[..., query_cols + keyval_cols :].reshape(local_rows, steps, KVH, HD)
    places = positions.astype(jnp.float32)[:, None] + jnp.arange(steps, dtype=jnp.float32)[None, :]
    turned_queries = rotate(queries.astype(jnp.float32), places).astype(jnp.bfloat16)
    turned_keys = rotate(fresh_keys.astype(jnp.float32), places).astype(jnp.bfloat16)
    new_keyvals = jnp.stack(
        [
            turned_keys.reshape(local_rows, steps, KVH * HD),
            fresh_values.reshape(local_rows, steps, KVH * HD),
        ]
    )
    attended = attend(
        turned_queries, turned_keys, fresh_values, cache_keys, cache_values, cache_lengths
    )
    returned = lax.all_to_all(attended, "gy", split_axis=2, concat_axis=0, tiled=True)
    rows_all = lax.all_gather(returned, "gx", axis=0, tiled=True)
    head_cols = rows_all.shape[2]
    all_rows = rows_all.shape[0]
    out_rows_here = all_rows // head_parts
    product = jnp.dot(
        rows_all.reshape(lax.axis_size("gy") * out_rows_here * steps, head_cols),
        w_out,
        preferred_element_type=jnp.float32,
    )
    branch = lax.psum_scatter(
        product.reshape(lax.axis_size("gy") * out_rows_here, steps, -1),
        "gy",
        scatter_dimension=0,
        tiled=True,
    )
    return (branch.astype(jnp.bfloat16), new_keyvals)


def peer_id(axis, index):
    return {axis: index}


def remote(src, dst, send_sem, recv_sem, axis, index):
    return pltpu.make_async_remote_copy(
        src_ref=src,
        dst_ref=dst,
        send_sem=send_sem,
        recv_sem=recv_sem,
        device_id=peer_id(axis, index),
        device_id_type=pl.DeviceIdType.MESH,
    )


def greet(x, y, nx, ny):
    barrier = pltpu.get_barrier_semaphore()
    for d in range(1, nx):
        pl.semaphore_signal(
            barrier, inc=1, device_id=peer_id("gx", lax.rem(x + d, nx)),
            device_id_type=pl.DeviceIdType.MESH,
        )
    for d in range(1, ny):
        pl.semaphore_signal(
            barrier, inc=1, device_id=peer_id("gy", lax.rem(y + d, ny)),
            device_id_type=pl.DeviceIdType.MESH,
        )
    pl.semaphore_wait(barrier, nx - 1 + ny - 1)


def layer_kernel(
    nx, ny, x_ref, gain_ref, len_ref, cos_ref, sin_ref, wq_hbm, wkv_hbm, key_hbm, val_hbm, wo_hbm,
    out_ref, kv_ref,
    xf, cosbuf, sinbuf, wq, wkv, xbuf, sqbuf, parts, rbuf, qbuf, kvbuf, sendbuf, landed,
    keys, vals, wo, att, abuf, fbuf, lbuf, prod, pbuf, qland, chip, zsend, zland,
    wq_sem, wkv_sem, sq_s, sq_r, g_s, g_r, rs_s, rs_r, a_s, a_r,
    key_sem, val_sem, wo_sem, b_s, b_r, l_s, l_r, c_s, c_r, z_s, z_r,
):
    x = lax.axis_index("gx")
    y = lax.axis_index("gy")
    nz = ny // 2
    z = y // 2
    c = lax.rem(y, 2)
    nblocks = wq.shape[0]
    bc = wq.shape[2]
    head = wkv.shape[2]
    chunk = rbuf.shape[2]
    no = wo.shape[0]
    oc = wo.shape[2]

    def load_q(j):
        cols = pl.ds(j * bc, bc) if isinstance(j, int) else pl.ds(pl.multiple_of(j * bc, bc), bc)
        return pltpu.make_async_copy(wq_hbm.at[:, cols], wq.at[j], wq_sem.at[j])

    def load_kv():
        return pltpu.make_async_copy(wkv_hbm, wkv, wkv_sem)

    load_kv().start()
    for j in range(nblocks):
        load_q(j).start()

    count = x_ref.shape[1]
    for i in range(x_ref.shape[0]):
        xf[count * i : count * (i + 1), :] = x_ref[i].astype(jnp.float32)
    features = xf[...]
    squares = jnp.sum(features * features, axis=-1, keepdims=True)
    sqbuf[0] = jnp.broadcast_to(squares, sqbuf.shape[1:])
    greet(x, y, nx, ny)
    sq_copies = [
        remote(sqbuf.at[0], sqbuf.at[d], sq_s.at[d - 1], sq_r.at[d - 1], "gx", lax.rem(x + d, nx))
        for d in range(1, nx)
    ]
    for copy in sq_copies:
        copy.start()
    for copy in sq_copies:
        copy.wait_recv()
    total = sqbuf[0]
    for d in range(1, nx):
        total = total + sqbuf[d]
    inverse = lax.rsqrt(total[:, :1] / D + norm_epsilon)
    normed = (
        features * inverse * gain_ref[...].astype(jnp.float32).reshape(1, features.shape[1])
    ).astype(jnp.bfloat16)
    half = xbuf.shape[3]
    xbuf[0, y] = normed

    def hop(t, block, k):
        dest = (y - 2, y + 2, y + 1 - 2 * c)[k]
        return remote(
            xbuf.at[t, block], xbuf.at[t, block], g_s.at[t, block, k], g_r.at[t, block], "gy", dest
        )

    def begin(t):
        @pl.when(z > 0)
        def _():
            hop(t, y, 0).start()

        @pl.when(z < nz - 1)
        def _():
            hop(t, y, 1).start()

        hop(t, y, 2).start()

    def forward(t, d):
        @pl.when(z - d >= 0)
        def _():
            block = y - 2 * d
            hop(t, block, 2).wait_recv()

            @pl.when(z < nz - 1)
            def _():
                hop(t, block, 1).start()

            hop(t, block, 2).start()

        @pl.when(z + d < nz)
        def _():
            block = y + 2 * d
            hop(t, block, 2).wait_recv()

            @pl.when(z > 0)
            def _():
                hop(t, block, 0).start()

            hop(t, block, 2).start()

    def from_pair(t):
        for zz in range(nz):
            hop(t, 2 * zz + 1 - c, 2).wait_recv()

    begin(0)
    for d in range(1, nz):
        forward(0, d)
    from_pair(0)

    def load_cache(g):
        cols = pl.ds(g * head, head) if isinstance(g, int) else pl.ds(pl.multiple_of(g * head, head), head)
        return (
            pltpu.make_async_copy(key_hbm.at[:, :, cols], keys.at[g], key_sem.at[g]),
            pltpu.make_async_copy(val_hbm.at[:, :, cols], vals.at[g], val_sem.at[g]),
        )

    def load_o(j):
        cols = pl.ds(j * oc, oc) if isinstance(j, int) else pl.ds(pl.multiple_of(j * oc, oc), oc)
        return pltpu.make_async_copy(wo_hbm.at[:, cols], wo.at[j], wo_sem.at[j])

    def rs(j, d):
        to = lax.rem(x + d, nx)
        rows = pl.ds(pl.multiple_of(to * chunk, chunk), chunk)
        return remote(
            parts.at[j, rows, :], rbuf.at[d - 1, j], rs_s.at[d - 1, j], rs_r.at[d - 1, j], "gx", to
        )

    tokens = xbuf.shape[1] * xbuf.shape[2]

    def times(t, weights):
        return jnp.dot(
            xbuf[t].reshape(tokens, half), weights, preferred_element_type=jnp.float32
        )

    load_kv().wait()
    for n in range(2):
        parts[nblocks, :, n * head : (n + 1) * head] = times(0, wkv[n])
    for d in range(1, nx):
        rs(nblocks, d).start()

    def block_step(j, carry):
        load_q(j).wait()
        parts[j] = times(0, wq[j])
        for d in range(1, nx):
            rs(j, d).start()
        for copy in load_cache(j):
            copy.start()
        return carry

    lax.fori_loop(0, nblocks, block_step, 0)

    own = pl.ds(pl.multiple_of(x * chunk, chunk), chunk)
    per_block = bc // head
    heads = nblocks * per_block
    kvbuf[...] = jnp.zeros_like(kvbuf)
    for j in [nblocks] + list(range(nblocks)):
        for d in range(1, nx):
            rs(j, d).wait_recv()
        summed = parts[j, own, :]
        for d in range(1, nx):
            summed = summed + rbuf[d - 1, j]
        for i in range(per_block):
            piece = summed[:, i * head : (i + 1) * head]
            if j < nblocks:
                qbuf[pl.ds(j * per_block + i, chunk, stride=heads), :] = piece
            else:
                kvbuf[pl.ds(i, chunk, stride=4), :] = piece
    local = chunk // ny
    sendbuf[:, : local * heads, :] = (
        qbuf[...].astype(jnp.bfloat16).reshape(ny, local * heads, head)
    )
    sendbuf[:, local * heads :, :] = kvbuf[...].astype(jnp.bfloat16).reshape(ny, local * 4, head)

    def a2a(d):
        to = lax.rem(y + d, ny)
        return remote(sendbuf.at[to], landed.at[y], a_s.at[d - 1], a_r.at[d - 1], "gy", to)

    for d in range(1, ny):
        a2a(d).start()
    landed[y] = sendbuf[y]

    for buf, first, last in ((cosbuf, 1.0, 1.0), (sinbuf, -1.0, 1.0)):
        table = cos_ref if buf is cosbuf else sin_ref
        lines = []
        for b in range(table.shape[0]):
            line = table[b]
            line = jnp.concatenate([line * first, line * last], axis=1)
            lines += [line[r : r + 1] for r in range(STEPS)]
        for r, line in enumerate(lines):
            buf[r * heads : (r + 1) * heads, :] = jnp.broadcast_to(line, (heads, head))
        tail = [jnp.broadcast_to(line, (4, head)) for line in lines]
        buf[local * heads :, :] = jnp.concatenate(tail, axis=0)

    def b2a(d):
        to = lax.rem(y + d, ny)
        return remote(att.at[to], abuf.at[y], b_s.at[d - 1], b_r.at[d - 1], "gy", to)

    def one_head(g, q_block, key, val):
        raw = q_block.astype(jnp.float32)
        swapped = jnp.concatenate([raw[:, head // 2 :], raw[:, : head // 2]], axis=1)
        turned = (raw * cosbuf[...] + swapped * sinbuf[...]).astype(jnp.bfloat16)
        turned_f = turned.astype(jnp.float32)
        slots = key.shape[1]
        group = heads
        count = STEPS * group
        scale = HD ** (-0.5)
        col = lax.broadcasted_iota(jnp.int32, (count, 4 * STEPS), 1)
        step = lax.broadcasted_iota(jnp.int32, (count, 4 * STEPS), 0) // group
        keep_new = (col % 4 == 0) & (col // 4 <= step)
        slot = lax.broadcasted_iota(jnp.int32, (count, slots), 1)
        keys_out, values_out, mixes = [], [], []
        for b in range(key.shape[0]):
            q = turned[b * count : (b + 1) * count]
            base = key.shape[0] * count + b * 4 * STEPS
            kv_turned = turned_f[base : base + 4 * STEPS]
            kv_raw = raw[base : base + 4 * STEPS]
            old = lax.dot_general(
                q, key[b], (((1,), (1,)), ((), ())), preferred_element_type=jnp.float32
            ) * scale
            new = lax.dot_general(
                q, kv_turned.astype(jnp.bfloat16), (((1,), (1,)), ((), ())),
                preferred_element_type=jnp.float32,
            ) * scale
            old = jnp.where(slot < len_ref[b], old, -1e30)
            new = jnp.where(keep_new, new, -1e30)
            highest = jnp.maximum(
                jnp.max(old, axis=-1, keepdims=True), jnp.max(new, axis=-1, keepdims=True)
            )
            old = jnp.exp(old - highest)
            new = jnp.exp(new - highest)
            denom = jnp.sum(old, axis=-1, keepdims=True) + jnp.sum(new, axis=-1, keepdims=True)
            mixed = jnp.dot(old.astype(jnp.bfloat16), val[b], preferred_element_type=jnp.float32)
            new = new.astype(jnp.bfloat16).astype(jnp.float32)
            for r in range(STEPS):
                mixed = mixed + new[:, 4 * r : 4 * r + 1] * kv_raw[4 * r + 1 : 4 * r + 2]
            for out, block, at in ((keys_out, kv_turned, 0), (values_out, kv_raw, 1)):
                lines = [block[4 * r + at : 4 * r + at + 1] for r in range(STEPS)]
                out.append(jnp.concatenate(lines, axis=0).astype(jnp.bfloat16))
            mixes.append((mixed / denom).astype(jnp.bfloat16))
        return jnp.concatenate(mixes, axis=0), (keys_out, values_out)

    def keep(g, mixed, fresh):
        att[g] = mixed
        for n in range(2):
            for b in range(kv_ref.shape[1]):
                kv_ref[n, b, :, pl.ds(pl.multiple_of(g * head, head), head)] = fresh[n][b]

    def two_heads(i, carry):
        first = lax.rem(y + 1 + 2 * i, ny)
        second = lax.rem(y + 2 + 2 * i, ny)
        a2a(ny - 1 - 2 * i).wait_recv()

        @pl.when(i < ny // 2 - 1)
        def _():
            a2a(ny - 2 - 2 * i).wait_recv()

        for g in (first, second):
            for copy in load_cache(g):
                copy.wait()
        loaded = [(g, landed[g], keys[g], vals[g]) for g in (first, second)]
        results = [one_head(*items) for items in loaded]
        keep(first, *results[0])
        keep(second, *results[1])
        b2a(2 * i + 1).start()

        @pl.when(i < ny // 2 - 1)
        def _():
            b2a(2 * i + 2).start()

        for n in range(per_turn):
            load_o(per_turn * i + n).start()
        return carry

    per_turn = no // (ny // 2)
    lax.fori_loop(0, ny // 2, two_heads, 0)
    abuf[y] = att[y]
    for d in range(1, ny):
        b2a(d).wait_recv()
    fbuf[...] = abuf[...].astype(jnp.float32).reshape(fbuf.shape)

    def gather(t, d):
        return remote(
            lbuf.at[t, x], lbuf.at[t, x], l_s.at[t, d - 1], l_r.at[t, d - 1], "gx", lax.rem(x + d, nx)
        )

    for h in range(heads):
        lbuf[0, x, :, h * head : (h + 1) * head] = fbuf[
            pl.ds(h, chunk, stride=heads), :
        ].astype(jnp.bfloat16)
    for d in range(1, nx):
        gather(0, d).start()
    for d in range(1, nx):
        gather(0, d).wait_recv()

    def pair(j):
        return remote(pbuf.at[j], qland.at[j], c_s.at[j], c_r.at[j], "gy", y + 1 - 2 * c)

    def along(j, d):
        to = lax.rem(z + d, nz)
        return remote(
            zsend.at[j, to], zland.at[d - 1, j], z_s.at[d - 1, j], z_r.at[d - 1, j], "gy", 2 * to + c
        )

    def pass_on(j):
        pair(j).wait_recv()
        chip[j] = prod[j, :, c] + qland[j].astype(jnp.float32)
        zsend[j] = chip[j].astype(jnp.bfloat16)
        for d in range(1, nz):
            along(j, d).start()

    def out_step(j, carry):
        load_o(j).wait()
        prod[j] = jnp.dot(
            lbuf[0].reshape(nx * chunk, lbuf.shape[3]), wo[j], preferred_element_type=jnp.float32
        ).reshape(prod.shape[1:])
        pbuf[j] = prod[j, :, 1 - c].astype(jnp.bfloat16)
        pair(j).start()

        @pl.when(j > 0)
        def _():
            pass_on(j - 1)

        return carry

    lax.fori_loop(0, no, out_step, 0)
    pass_on(no - 1)
    for j in range(no):
        total = chip[j, z]
        for d in range(1, nz):
            along(j, d).wait_recv()
            total = total + zland[d - 1, j].astype(jnp.float32)
        for i in range(out_ref.shape[0]):
            out_ref[i, :, j * oc : (j + 1) * oc] = total[count * i : count * (i + 1)].astype(
                jnp.bfloat16
            )

    for d in range(1, ny):
        b2a(d).wait_send()
    for d in range(1, nx):
        gather(0, d).wait_send()

    def done(j, carry):
        pair(j).wait_send()
        for d in range(1, nz):
            along(j, d).wait_send()
        return carry

    lax.fori_loop(0, no, done, 0)

    for copy in sq_copies:
        copy.wait_send()
    for t in range(1):
        for zz in range(nz):
            block = 2 * zz + c
            hop(t, block, 2).wait_send()

            @pl.when((zz >= z) & (z > 0))
            def _():
                hop(t, block, 0).wait_send()

            @pl.when((zz <= z) & (z < nz - 1))
            def _():
                hop(t, block, 1).wait_send()

    def rs_done(j, carry):
        for d in range(1, nx):
            rs(j, d).wait_send()
        return carry

    lax.fori_loop(0, nblocks + 1, rs_done, 0)
    for d in range(1, ny):
        a2a(d).wait_send()


def write_kernel(branch_ref, kv_ref, branch_out, kv_out):
    branch_out[...] = branch_ref[...]
    kv_out[...] = kv_ref[...]


def with_kernels(
    hidden, norm_gain, w_query, w_keyval, w_out, cache_keys, cache_values, cache_lengths, positions
):
    nx = lax.axis_size("gx")
    ny = lax.axis_size("gy")
    nz = ny // 2
    rows, steps, width = hidden.shape
    mine = rows * steps
    tokens = ny * mine
    chunk = tokens // nx
    local_rows = cache_keys.shape[0]
    local = local_rows * steps
    cols = w_query.shape[1]
    heads = cols // HD
    bc = 256
    nq = cols // bc
    packed = local * heads + local * 4
    vmem = pl.BlockSpec(memory_space=pltpu.VMEM)
    hbm = pl.BlockSpec(memory_space=pl.ANY)
    dma = pltpu.SemaphoreType.DMA
    places = positions.astype(jnp.float32)[:, None] + jnp.arange(steps, dtype=jnp.float32)[None, :]
    angles = places[..., None] * rope_rates()
    slots = cache_keys.shape[1]
    oc = 512
    no = w_out.shape[1] // oc
    made = pl.pallas_call(
        functools.partial(layer_kernel, nx, ny),
        out_shape=(
            jax.ShapeDtypeStruct((rows, steps, w_out.shape[1]), jnp.bfloat16),
            jax.ShapeDtypeStruct((2, local_rows, steps, KVH * HD), jnp.bfloat16),
        ),
        in_specs=[vmem, vmem, pl.BlockSpec(memory_space=pltpu.SMEM), vmem, vmem] + [hbm] * 5,
        out_specs=(vmem, vmem),
        scratch_shapes=[
            pltpu.VMEM((mine, width), jnp.float32),
            pltpu.VMEM((packed, HD), jnp.float32),
            pltpu.VMEM((packed, HD), jnp.float32),
            pltpu.VMEM((nq, width, bc), jnp.bfloat16),
            pltpu.VMEM(w_keyval.shape, jnp.bfloat16),
            pltpu.VMEM((1, ny, mine, width), jnp.bfloat16),
            pltpu.VMEM((nx, mine, 128), jnp.float32),
            pltpu.VMEM((nq + 1, tokens, bc), jnp.float32),
            pltpu.VMEM((nx - 1, nq + 1, chunk, bc), jnp.float32),
            pltpu.VMEM((chunk * heads, HD), jnp.float32),
            pltpu.VMEM((chunk * 4, HD), jnp.float32),
            pltpu.VMEM((ny, packed, HD), jnp.bfloat16),
            pltpu.VMEM((ny, packed, HD), jnp.bfloat16),
            pltpu.VMEM((ny, local_rows, slots, HD), jnp.bfloat16),
            pltpu.VMEM((ny, local_rows, slots, HD), jnp.bfloat16),
            pltpu.VMEM((no, cols, oc), jnp.bfloat16),
            pltpu.VMEM((ny, local * heads, HD), jnp.bfloat16),
            pltpu.VMEM((ny, local * heads, HD), jnp.bfloat16),
            pltpu.VMEM((chunk * heads, HD), jnp.float32),
            pltpu.VMEM((1, nx, chunk, cols), jnp.bfloat16),
            pltpu.VMEM((no, nz, 2, mine, oc), jnp.float32),
            pltpu.VMEM((no, nz, mine, oc), jnp.bfloat16),
            pltpu.VMEM((no, nz, mine, oc), jnp.bfloat16),
            pltpu.VMEM((no, nz, mine, oc), jnp.float32),
            pltpu.VMEM((no, nz, mine, oc), jnp.bfloat16),
            pltpu.VMEM((nz - 1, no, mine, oc), jnp.bfloat16),
            dma((nq,)),
            dma(()),
            dma((nx - 1,)),
            dma((nx - 1,)),
            dma((1, ny, 3)),
            dma((1, ny)),
            dma((nx - 1, nq + 1)),
            dma((nx - 1, nq + 1)),
            dma((ny - 1,)),
            dma((ny - 1,)),
            dma((ny,)),
            dma((ny,)),
            dma((no,)),
            dma((ny - 1,)),
            dma((ny - 1,)),
            dma((1, nx - 1)),
            dma((1, nx - 1)),
            dma((no,)),
            dma((no,)),
            dma((nz - 1, no)),
            dma((nz - 1, no)),
        ],
        compiler_params=pltpu.CompilerParams(
            collective_id=0, has_side_effects=True, vmem_limit_bytes=60 * 1024 * 1024
        ),
        name="layer",
    )(
        hidden, norm_gain, cache_lengths, jnp.cos(angles), jnp.sin(angles),
        w_query, w_keyval, cache_keys, cache_values, w_out,
    )
    return pl.pallas_call(
        write_kernel,
        out_shape=tuple(jax.ShapeDtypeStruct(item.shape, item.dtype) for item in made),
        in_specs=[vmem, vmem],
        out_specs=(vmem, vmem),
        name="write",
    )(*made)


def on_device(*args):
    hidden, _, w_query, w_keyval, w_out, cache_keys = args[:6]
    nx, ny = lax.axis_size("gx"), lax.axis_size("gy")
    local = cache_keys.shape[0] * hidden.shape[1]
    fits = (
        w_keyval.shape[2] == HD
        and ny == KVH
        and hidden.shape[1] == STEPS
        and hidden.shape[0] * hidden.shape[1] % 16 == 0
        and local == 4
        and w_query.shape[1] % 256 == 0
        and w_out.shape[1] % 512 == 0
        and nx > 1
        and w_query.shape[1] // 256 == ny
        and (w_out.shape[1] // 512) % (ny // 2) == 0
    )
    return with_kernels(*args) if fits else plain(*args)


def solution(mesh):
    return jax.shard_map(
        on_device,
        mesh=mesh,
        in_specs=(
            P("gy", None, "gx"),
            P("gx"),
            P("gx", "gy"),
            P(None, "gx", "gy"),
            P("gy", "gx"),
            P(("gx", "gy"), None, None),
            P(("gx", "gy"), None, None),
            P(("gx", "gy")),
            P(("gx", "gy")),
        ),
        out_specs=(P("gy", None, "gx"), P(None, ("gx", "gy"), None, None)),
        check_vma=False,
    )
```

```python
import functools
import math

import jax
import jax.numpy as jnp
from jax import lax
from jax.experimental import pallas as pl
from jax.experimental.pallas import tpu as pltpu
from jax.sharding import PartitionSpec as P

D = 16384
HQ = 128
KVH = 8
HD = 128
STEPS = 2


norm_epsilon = 1e-05


def rope_rates():
    index = jnp.arange(HD // 2, dtype=jnp.float32)
    rates = 1.0 / jnp.power(500000.0, 2.0 * index / HD)
    wavelength = 2.0 * math.pi / rates
    smooth = (8192.0 / wavelength - 1.0) / 3.0
    blended = (1.0 - smooth) * rates / 8.0 + smooth * rates
    return jnp.where(
        wavelength > 8192.0, rates / 8.0, jnp.where(wavelength < 2048.0, rates, blended)
    )


def rotate(vectors, places):
    angles = places[..., None, None] * rope_rates()
    half_size = vectors.shape[-1] // 2
    first_half = vectors[..., :half_size]
    second_half = vectors[..., half_size:]
    cosine = jnp.cos(angles)
    sine = jnp.sin(angles)
    return jnp.concatenate(
        [first_half * cosine - second_half * sine, second_half * cosine + first_half * sine],
        axis=-1,
    )


def attend(queries, fresh_keys, fresh_values, cached_keys, cached_values, lengths):
    rows, steps = (queries.shape[0], queries.shape[1])
    slots = cached_keys.shape[1]
    grouped = queries.reshape(rows, steps, KVH, HQ // KVH, HD)
    old_keys = cached_keys.reshape(rows, slots, KVH, HD)
    old_values = cached_values.reshape(rows, slots, KVH, HD)
    score_scale = HD ** (-0.5)
    cached = (
        jnp.einsum("bskgd,btkd->bskgt", grouped, old_keys, preferred_element_type=jnp.float32)
        * score_scale
    )
    fresh = (
        jnp.einsum("bskgd,brkd->bskgr", grouped, fresh_keys, preferred_element_type=jnp.float32)
        * score_scale
    )
    slot_valid = jnp.arange(slots)[None, :] < lengths[:, None]
    step_valid = jnp.arange(steps)[None, :] <= jnp.arange(steps)[:, None]
    cached = jnp.where(slot_valid[:, None, None, None, :], cached, -1e30)
    fresh = jnp.where(step_valid[None, :, None, None, :], fresh, -1e30)
    highest = jnp.maximum(jnp.max(cached, axis=-1), jnp.max(fresh, axis=-1))[..., None]
    weights_old = jnp.exp(cached - highest)
    weights_new = jnp.exp(fresh - highest)
    denom = jnp.sum(weights_old, axis=-1) + jnp.sum(weights_new, axis=-1)
    mixed = jnp.einsum(
        "bskgt,btkd->bskgd",
        weights_old.astype(jnp.bfloat16),
        old_values,
        preferred_element_type=jnp.float32,
    )
    mixed = mixed + jnp.einsum(
        "bskgr,brkd->bskgd",
        weights_new.astype(jnp.bfloat16),
        fresh_values,
        preferred_element_type=jnp.float32,
    )
    return (mixed / denom[..., None]).astype(jnp.bfloat16).reshape(rows, steps, HQ * HD)


def plain(
    hidden, norm_gain, w_query, w_keyval, w_out, cache_keys, cache_values, cache_lengths, positions
):
    steps = hidden.shape[1]
    features = hidden.astype(jnp.float32)
    squares = jnp.sum(features * features, axis=-1)
    square_sums = lax.psum(squares, "gx")
    inverse = lax.rsqrt(square_sums / D + norm_epsilon)
    normed = (features * inverse[..., None] * norm_gain.astype(jnp.float32)).astype(jnp.bfloat16)
    shard_rows = lax.all_gather(normed, "gy", axis=0, tiled=True)
    flattened = shard_rows.reshape(-1, shard_rows.shape[2])
    products = [
        jnp.dot(flattened, w_query, preferred_element_type=jnp.float32),
        jnp.dot(flattened, w_keyval[0], preferred_element_type=jnp.float32),
        jnp.dot(flattened, w_keyval[1], preferred_element_type=jnp.float32),
    ]
    partial_sums = jnp.concatenate(products, axis=-1).reshape(shard_rows.shape[0], steps, -1)
    width_parts = lax.axis_size("gx")
    head_parts = lax.axis_size("gy")
    block_rows = partial_sums.shape[0] // width_parts
    summed = lax.psum(partial_sums, "gx")
    summed = lax.dynamic_slice_in_dim(summed, lax.axis_index("gx") * block_rows, block_rows, 0)
    own_rows = summed.astype(jnp.bfloat16)
    arrived = lax.all_to_all(own_rows, "gy", split_axis=0, concat_axis=2, tiled=True)
    local_rows = arrived.shape[0]
    pieces = arrived.reshape(local_rows, steps, head_parts, -1)
    query_cols = w_query.shape[1]
    keyval_cols = w_keyval.shape[2]
    queries = pieces[..., :query_cols].reshape(local_rows, steps, HQ, HD)
    fresh_keys = pieces[..., query_cols : query_cols + keyval_cols].reshape(
        local_rows, steps, KVH, HD
    )
    fresh_values = pieces[..., query_cols + keyval_cols :].reshape(local_rows, steps, KVH, HD)
    places = positions.astype(jnp.float32)[:, None] + jnp.arange(steps, dtype=jnp.float32)[None, :]
    turned_queries = rotate(queries.astype(jnp.float32), places).astype(jnp.bfloat16)
    turned_keys = rotate(fresh_keys.astype(jnp.float32), places).astype(jnp.bfloat16)
    new_keyvals = jnp.stack(
        [
            turned_keys.reshape(local_rows, steps, KVH * HD),
            fresh_values.reshape(local_rows, steps, KVH * HD),
        ]
    )
    attended = attend(
        turned_queries, turned_keys, fresh_values, cache_keys, cache_values, cache_lengths
    )
    returned = lax.all_to_all(attended, "gy", split_axis=2, concat_axis=0, tiled=True)
    rows_all = lax.all_gather(returned, "gx", axis=0, tiled=True)
    head_cols = rows_all.shape[2]
    all_rows = rows_all.shape[0]
    out_rows_here = all_rows // head_parts
    product = jnp.dot(
        rows_all.reshape(lax.axis_size("gy") * out_rows_here * steps, head_cols),
        w_out,
        preferred_element_type=jnp.float32,
    )
    branch = lax.psum_scatter(
        product.reshape(lax.axis_size("gy") * out_rows_here, steps, -1),
        "gy",
        scatter_dimension=0,
        tiled=True,
    )
    return (branch.astype(jnp.bfloat16), new_keyvals)


def peer_id(axis, index):
    return {axis: index}


def remote(src, dst, send_sem, recv_sem, axis, index):
    return pltpu.make_async_remote_copy(
        src_ref=src,
        dst_ref=dst,
        send_sem=send_sem,
        recv_sem=recv_sem,
        device_id=peer_id(axis, index),
        device_id_type=pl.DeviceIdType.MESH,
    )


def greet(x, y, nx, ny):
    barrier = pltpu.get_barrier_semaphore()
    for d in range(1, nx):
        pl.semaphore_signal(
            barrier, inc=1, device_id=peer_id("gx", lax.rem(x + d, nx)),
            device_id_type=pl.DeviceIdType.MESH,
        )
    for d in range(1, ny):
        pl.semaphore_signal(
            barrier, inc=1, device_id=peer_id("gy", lax.rem(y + d, ny)),
            device_id_type=pl.DeviceIdType.MESH,
        )
    pl.semaphore_wait(barrier, nx - 1 + ny - 1)


def layer_kernel(
    nx, ny, x_ref, gain_ref, len_ref, cos_ref, sin_ref, wq_hbm, wkv_hbm, key_hbm, val_hbm, wo_hbm,
    out_ref, kv_ref,
    xf, cosbuf, sinbuf, wq, wkv, xbuf, sqbuf, parts, rbuf, qbuf, kvbuf, sendbuf, landed,
    keys, vals, wo, att, abuf, fbuf, lbuf, prod, pbuf, qland, chip, zsend, zland,
    wq_sem, wkv_sem, sq_s, sq_r, g_s, g_r, rs_s, rs_r, a_s, a_r,
    key_sem, val_sem, wo_sem, b_s, b_r, l_s, l_r, c_s, c_r, z_s, z_r,
):
    x = lax.axis_index("gx")
    y = lax.axis_index("gy")
    nz = ny // 2
    z = y // 2
    c = lax.rem(y, 2)
    nblocks = wq.shape[0]
    bc = wq.shape[2]
    head = wkv.shape[2]
    chunk = rbuf.shape[2]
    no = wo.shape[0]
    oc = wo.shape[2]

    def load_q(j):
        cols = pl.ds(j * bc, bc) if isinstance(j, int) else pl.ds(pl.multiple_of(j * bc, bc), bc)
        return pltpu.make_async_copy(wq_hbm.at[:, cols], wq.at[j], wq_sem.at[j])

    def load_kv():
        return pltpu.make_async_copy(wkv_hbm, wkv, wkv_sem)

    load_kv().start()
    for j in range(nblocks):
        load_q(j).start()

    count = x_ref.shape[1]
    for i in range(x_ref.shape[0]):
        xf[count * i : count * (i + 1), :] = x_ref[i].astype(jnp.float32)
    features = xf[...]
    squares = jnp.sum(features * features, axis=-1, keepdims=True)
    sqbuf[0] = jnp.broadcast_to(squares, sqbuf.shape[1:])
    greet(x, y, nx, ny)
    sq_copies = [
        remote(sqbuf.at[0], sqbuf.at[d], sq_s.at[d - 1], sq_r.at[d - 1], "gx", lax.rem(x + d, nx))
        for d in range(1, nx)
    ]
    for copy in sq_copies:
        copy.start()
    for copy in sq_copies:
        copy.wait_recv()
    total = sqbuf[0]
    for d in range(1, nx):
        total = total + sqbuf[d]
    inverse = lax.rsqrt(total[:, :1] / D + norm_epsilon)
    normed = (
        features * inverse * gain_ref[...].astype(jnp.float32).reshape(1, features.shape[1])
    ).astype(jnp.bfloat16)
    half = xbuf.shape[3] // 2
    xbuf[0, y] = normed

    def hop(t, block, k):
        dest = (y - 2, y + 2, y + 1 - 2 * c)[k]
        piece = xbuf.at[0, block, :, pl.ds(t * half, half)]
        return remote(piece, piece, g_s.at[t, block, k], g_r.at[t, block], "gy", dest)

    def begin(t):
        @pl.when(z > 0)
        def _():
            hop(t, y, 0).start()

        @pl.when(z < nz - 1)
        def _():
            hop(t, y, 1).start()

        hop(t, y, 2).start()

    def forward(t, d):
        @pl.when(z - d >= 0)
        def _():
            block = y - 2 * d
            hop(t, block, 2).wait_recv()

            @pl.when(z < nz - 1)
            def _():
                hop(t, block, 1).start()

            hop(t, block, 2).start()

        @pl.when(z + d < nz)
        def _():
            block = y + 2 * d
            hop(t, block, 2).wait_recv()

            @pl.when(z > 0)
            def _():
                hop(t, block, 0).start()

            hop(t, block, 2).start()

    def from_pair(t):
        for zz in range(nz):
            hop(t, 2 * zz + 1 - c, 2).wait_recv()

    for t in range(2):
        begin(t)
    for d in range(1, nz):
        for t in range(2):
            forward(t, d)
    for t in range(2):
        from_pair(t)

    def load_cache(g):
        cols = pl.ds(g * head, head) if isinstance(g, int) else pl.ds(pl.multiple_of(g * head, head), head)
        return (
            pltpu.make_async_copy(key_hbm.at[:, :, cols], keys.at[g], key_sem.at[g]),
            pltpu.make_async_copy(val_hbm.at[:, :, cols], vals.at[g], val_sem.at[g]),
        )

    def load_o(j):
        cols = pl.ds(j * oc, oc) if isinstance(j, int) else pl.ds(pl.multiple_of(j * oc, oc), oc)
        return pltpu.make_async_copy(wo_hbm.at[:, cols], wo.at[j], wo_sem.at[j])

    def rs(j, d):
        to = lax.rem(x + d, nx)
        rows = pl.ds(pl.multiple_of(to * chunk, chunk), chunk)
        return remote(
            parts.at[j, rows, :], rbuf.at[d - 1, j], rs_s.at[d - 1, j], rs_r.at[d - 1, j], "gx", to
        )

    tokens = xbuf.shape[1] * xbuf.shape[2]

    def times(t, weights):
        return jnp.dot(
            xbuf[t].reshape(tokens, xbuf.shape[3]), weights, preferred_element_type=jnp.float32
        )

    load_kv().wait()
    for n in range(2):
        parts[nblocks, :, n * head : (n + 1) * head] = times(0, wkv[n])
    for d in range(1, nx):
        rs(nblocks, d).start()

    def block_step(j, carry):
        load_q(j).wait()
        parts[j] = times(0, wq[j])
        for d in range(1, nx):
            rs(j, d).start()
        for copy in load_cache(j):
            copy.start()
        return carry

    lax.fori_loop(0, nblocks, block_step, 0)

    own = pl.ds(pl.multiple_of(x * chunk, chunk), chunk)
    per_block = bc // head
    heads = nblocks * per_block
    kvbuf[...] = jnp.zeros_like(kvbuf)
    for j in [nblocks] + list(range(nblocks)):
        for d in range(1, nx):
            rs(j, d).wait_recv()
        summed = parts[j, own, :]
        for d in range(1, nx):
            summed = summed + rbuf[d - 1, j]
        for i in range(per_block):
            piece = summed[:, i * head : (i + 1) * head]
            if j < nblocks:
                qbuf[pl.ds(j * per_block + i, chunk, stride=heads), :] = piece
            else:
                kvbuf[pl.ds(i, chunk, stride=4), :] = piece
    local = chunk // ny
    sendbuf[:, : local * heads, :] = (
        qbuf[...].astype(jnp.bfloat16).reshape(ny, local * heads, head)
    )
    sendbuf[:, local * heads :, :] = kvbuf[...].astype(jnp.bfloat16).reshape(ny, local * 4, head)

    def a2a(d):
        to = lax.rem(y + d, ny)
        return remote(sendbuf.at[to], landed.at[y], a_s.at[d - 1], a_r.at[d - 1], "gy", to)

    for d in range(1, ny):
        a2a(d).start()
    landed[y] = sendbuf[y]

    for buf, first, last in ((cosbuf, 1.0, 1.0), (sinbuf, -1.0, 1.0)):
        table = cos_ref if buf is cosbuf else sin_ref
        lines = []
        for b in range(table.shape[0]):
            line = table[b]
            line = jnp.concatenate([line * first, line * last], axis=1)
            lines += [line[r : r + 1] for r in range(STEPS)]
        for r, line in enumerate(lines):
            buf[r * heads : (r + 1) * heads, :] = jnp.broadcast_to(line, (heads, head))
        tail = [jnp.broadcast_to(line, (4, head)) for line in lines]
        buf[local * heads :, :] = jnp.concatenate(tail, axis=0)

    def b2a(d):
        to = lax.rem(y + d, ny)
        return remote(att.at[to], abuf.at[y], b_s.at[d - 1], b_r.at[d - 1], "gy", to)

    def one_head(g, q_block, key, val):
        raw = q_block.astype(jnp.float32)
        swapped = jnp.concatenate([raw[:, head // 2 :], raw[:, : head // 2]], axis=1)
        turned = (raw * cosbuf[...] + swapped * sinbuf[...]).astype(jnp.bfloat16)
        turned_f = turned.astype(jnp.float32)
        slots = key.shape[1]
        group = heads
        count = STEPS * group
        scale = HD ** (-0.5)
        col = lax.broadcasted_iota(jnp.int32, (count, 4 * STEPS), 1)
        step = lax.broadcasted_iota(jnp.int32, (count, 4 * STEPS), 0) // group
        keep_new = (col % 4 == 0) & (col // 4 <= step)
        slot = lax.broadcasted_iota(jnp.int32, (count, slots), 1)
        keys_out, values_out, mixes = [], [], []
        for b in range(key.shape[0]):
            q = turned[b * count : (b + 1) * count]
            base = key.shape[0] * count + b * 4 * STEPS
            kv_turned = turned_f[base : base + 4 * STEPS]
            kv_raw = raw[base : base + 4 * STEPS]
            old = lax.dot_general(
                q, key[b], (((1,), (1,)), ((), ())), preferred_element_type=jnp.float32
            ) * scale
            new = lax.dot_general(
                q, kv_turned.astype(jnp.bfloat16), (((1,), (1,)), ((), ())),
                preferred_element_type=jnp.float32,
            ) * scale
            old = jnp.where(slot < len_ref[b], old, -1e30)
            new = jnp.where(keep_new, new, -1e30)
            highest = jnp.maximum(
                jnp.max(old, axis=-1, keepdims=True), jnp.max(new, axis=-1, keepdims=True)
            )
            old = jnp.exp(old - highest)
            new = jnp.exp(new - highest)
            denom = jnp.sum(old, axis=-1, keepdims=True) + jnp.sum(new, axis=-1, keepdims=True)
            mixed = jnp.dot(old.astype(jnp.bfloat16), val[b], preferred_element_type=jnp.float32)
            new = new.astype(jnp.bfloat16).astype(jnp.float32)
            for r in range(STEPS):
                mixed = mixed + new[:, 4 * r : 4 * r + 1] * kv_raw[4 * r + 1 : 4 * r + 2]
            for out, block, at in ((keys_out, kv_turned, 0), (values_out, kv_raw, 1)):
                lines = [block[4 * r + at : 4 * r + at + 1] for r in range(STEPS)]
                out.append(jnp.concatenate(lines, axis=0).astype(jnp.bfloat16))
            mixes.append((mixed / denom).astype(jnp.bfloat16))
        return jnp.concatenate(mixes, axis=0), (keys_out, values_out)

    def keep(g, mixed, fresh):
        att[g] = mixed
        for n in range(2):
            for b in range(kv_ref.shape[1]):
                kv_ref[n, b, :, pl.ds(pl.multiple_of(g * head, head), head)] = fresh[n][b]

    turns = ny // 4
    per_turn = no // turns

    def four_heads(i, carry):
        each = [lax.rem(y + 1 + 4 * i + n, ny) for n in range(4)]
        for n in range(3):
            a2a(ny - 1 - 4 * i - n).wait_recv()

        @pl.when(i < turns - 1)
        def _():
            a2a(ny - 4 - 4 * i).wait_recv()

        for g in each:
            for copy in load_cache(g):
                copy.wait()
        loaded = [(g, landed[g], keys[g], vals[g]) for g in each]
        results = [one_head(*items) for items in loaded]
        for g, result in zip(each, results):
            keep(g, *result)
        for n in range(3):
            b2a(4 * i + n + 1).start()

        @pl.when(i < turns - 1)
        def _():
            b2a(4 * i + 4).start()

        for n in range(per_turn):
            load_o(per_turn * i + n).start()
        return carry

    lax.fori_loop(0, turns, four_heads, 0)
    abuf[y] = att[y]
    for d in range(1, ny):
        b2a(d).wait_recv()
    fbuf[...] = abuf[...].astype(jnp.float32).reshape(fbuf.shape)

    def gather(t, d):
        return remote(
            lbuf.at[t, x], lbuf.at[t, x], l_s.at[t, d - 1], l_r.at[t, d - 1], "gx", lax.rem(x + d, nx)
        )

    for h in range(heads):
        lbuf[0, x, :, h * head : (h + 1) * head] = fbuf[
            pl.ds(h, chunk, stride=heads), :
        ].astype(jnp.bfloat16)
    for d in range(1, nx):
        gather(0, d).start()
    for d in range(1, nx):
        gather(0, d).wait_recv()

    def pair(j):
        return remote(pbuf.at[j], qland.at[j], c_s.at[j], c_r.at[j], "gy", y + 1 - 2 * c)

    def along(j, d):
        to = lax.rem(z + d, nz)
        return remote(
            zsend.at[j, to], zland.at[d - 1, j], z_s.at[d - 1, j], z_r.at[d - 1, j], "gy", 2 * to + c
        )

    def pass_on(j):
        pair(j).wait_recv()
        chip[j] = prod[j, :, c] + qland[j].astype(jnp.float32)
        zsend[j] = chip[j].astype(jnp.bfloat16)
        for d in range(1, nz):
            along(j, d).start()

    def out_step(j, carry):
        load_o(j).wait()
        prod[j] = jnp.dot(
            lbuf[0].reshape(nx * chunk, lbuf.shape[3]), wo[j], preferred_element_type=jnp.float32
        ).reshape(prod.shape[1:])
        pbuf[j] = prod[j, :, 1 - c].astype(jnp.bfloat16)
        pair(j).start()

        @pl.when(j > 0)
        def _():
            pass_on(j - 1)

        return carry

    lax.fori_loop(0, no, out_step, 0)
    pass_on(no - 1)
    for j in range(no):
        total = chip[j, z]
        for d in range(1, nz):
            along(j, d).wait_recv()
            total = total + zland[d - 1, j].astype(jnp.float32)
        for i in range(out_ref.shape[0]):
            out_ref[i, :, j * oc : (j + 1) * oc] = total[count * i : count * (i + 1)].astype(
                jnp.bfloat16
            )

    for d in range(1, ny):
        b2a(d).wait_send()
    for d in range(1, nx):
        gather(0, d).wait_send()

    def done(j, carry):
        pair(j).wait_send()
        for d in range(1, nz):
            along(j, d).wait_send()
        return carry

    lax.fori_loop(0, no, done, 0)

    for copy in sq_copies:
        copy.wait_send()
    for t in range(2):
        for zz in range(nz):
            block = 2 * zz + c
            hop(t, block, 2).wait_send()

            @pl.when((zz >= z) & (z > 0))
            def _():
                hop(t, block, 0).wait_send()

            @pl.when((zz <= z) & (z < nz - 1))
            def _():
                hop(t, block, 1).wait_send()

    def rs_done(j, carry):
        for d in range(1, nx):
            rs(j, d).wait_send()
        return carry

    lax.fori_loop(0, nblocks + 1, rs_done, 0)
    for d in range(1, ny):
        a2a(d).wait_send()


def write_kernel(branch_ref, kv_ref, branch_out, kv_out):
    branch_out[...] = branch_ref[...]
    kv_out[...] = kv_ref[...]


def with_kernels(
    hidden, norm_gain, w_query, w_keyval, w_out, cache_keys, cache_values, cache_lengths, positions
):
    nx = lax.axis_size("gx")
    ny = lax.axis_size("gy")
    nz = ny // 2
    rows, steps, width = hidden.shape
    mine = rows * steps
    tokens = ny * mine
    chunk = tokens // nx
    local_rows = cache_keys.shape[0]
    local = local_rows * steps
    cols = w_query.shape[1]
    heads = cols // HD
    bc = 256
    nq = cols // bc
    packed = local * heads + local * 4
    vmem = pl.BlockSpec(memory_space=pltpu.VMEM)
    hbm = pl.BlockSpec(memory_space=pl.ANY)
    dma = pltpu.SemaphoreType.DMA
    places = positions.astype(jnp.float32)[:, None] + jnp.arange(steps, dtype=jnp.float32)[None, :]
    angles = places[..., None] * rope_rates()
    slots = cache_keys.shape[1]
    oc = 512
    no = w_out.shape[1] // oc
    made = pl.pallas_call(
        functools.partial(layer_kernel, nx, ny),
        out_shape=(
            jax.ShapeDtypeStruct((rows, steps, w_out.shape[1]), jnp.bfloat16),
            jax.ShapeDtypeStruct((2, local_rows, steps, KVH * HD), jnp.bfloat16),
        ),
        in_specs=[vmem, vmem, pl.BlockSpec(memory_space=pltpu.SMEM), vmem, vmem] + [hbm] * 5,
        out_specs=(vmem, vmem),
        scratch_shapes=[
            pltpu.VMEM((mine, width), jnp.float32),
            pltpu.VMEM((packed, HD), jnp.float32),
            pltpu.VMEM((packed, HD), jnp.float32),
            pltpu.VMEM((nq, width, bc), jnp.bfloat16),
            pltpu.VMEM(w_keyval.shape, jnp.bfloat16),
            pltpu.VMEM((1, ny, mine, width), jnp.bfloat16),
            pltpu.VMEM((nx, mine, 128), jnp.float32),
            pltpu.VMEM((nq + 1, tokens, bc), jnp.float32),
            pltpu.VMEM((nx - 1, nq + 1, chunk, bc), jnp.float32),
            pltpu.VMEM((chunk * heads, HD), jnp.float32),
            pltpu.VMEM((chunk * 4, HD), jnp.float32),
            pltpu.VMEM((ny, packed, HD), jnp.bfloat16),
            pltpu.VMEM((ny, packed, HD), jnp.bfloat16),
            pltpu.VMEM((ny, local_rows, slots, HD), jnp.bfloat16),
            pltpu.VMEM((ny, local_rows, slots, HD), jnp.bfloat16),
            pltpu.VMEM((no, cols, oc), jnp.bfloat16),
            pltpu.VMEM((ny, local * heads, HD), jnp.bfloat16),
            pltpu.VMEM((ny, local * heads, HD), jnp.bfloat16),
            pltpu.VMEM((chunk * heads, HD), jnp.float32),
            pltpu.VMEM((1, nx, chunk, cols), jnp.bfloat16),
            pltpu.VMEM((no, nz, 2, mine, oc), jnp.float32),
            pltpu.VMEM((no, nz, mine, oc), jnp.bfloat16),
            pltpu.VMEM((no, nz, mine, oc), jnp.bfloat16),
            pltpu.VMEM((no, nz, mine, oc), jnp.float32),
            pltpu.VMEM((no, nz, mine, oc), jnp.bfloat16),
            pltpu.VMEM((nz - 1, no, mine, oc), jnp.bfloat16),
            dma((nq,)),
            dma(()),
            dma((nx - 1,)),
            dma((nx - 1,)),
            dma((2, ny, 3)),
            dma((2, ny)),
            dma((nx - 1, nq + 1)),
            dma((nx - 1, nq + 1)),
            dma((ny - 1,)),
            dma((ny - 1,)),
            dma((ny,)),
            dma((ny,)),
            dma((no,)),
            dma((ny - 1,)),
            dma((ny - 1,)),
            dma((1, nx - 1)),
            dma((1, nx - 1)),
            dma((no,)),
            dma((no,)),
            dma((nz - 1, no)),
            dma((nz - 1, no)),
        ],
        compiler_params=pltpu.CompilerParams(
            collective_id=0, has_side_effects=True, vmem_limit_bytes=60 * 1024 * 1024
        ),
        name="layer",
    )(
        hidden, norm_gain, cache_lengths, jnp.cos(angles), jnp.sin(angles),
        w_query, w_keyval, cache_keys, cache_values, w_out,
    )
    return pl.pallas_call(
        write_kernel,
        out_shape=tuple(jax.ShapeDtypeStruct(item.shape, item.dtype) for item in made),
        in_specs=[vmem, vmem],
        out_specs=(vmem, vmem),
        name="write",
    )(*made)


def on_device(*args):
    hidden, _, w_query, w_keyval, w_out, cache_keys = args[:6]
    nx, ny = lax.axis_size("gx"), lax.axis_size("gy")
    local = cache_keys.shape[0] * hidden.shape[1]
    fits = (
        w_keyval.shape[2] == HD
        and ny == KVH
        and hidden.shape[1] == STEPS
        and hidden.shape[0] * hidden.shape[1] % 16 == 0
        and local == 4
        and w_query.shape[1] % 256 == 0
        and w_out.shape[1] % 512 == 0
        and nx > 1
        and w_query.shape[1] // 256 == ny
        and (w_out.shape[1] // 512) % (ny // 4) == 0
    )
    return with_kernels(*args) if fits else plain(*args)


def solution(mesh):
    return jax.shard_map(
        on_device,
        mesh=mesh,
        in_specs=(
            P("gy", None, "gx"),
            P("gx"),
            P("gx", "gy"),
            P(None, "gx", "gy"),
            P("gy", "gx"),
            P(("gx", "gy"), None, None),
            P(("gx", "gy"), None, None),
            P(("gx", "gy")),
            P(("gx", "gy")),
        ),
        out_specs=(P("gy", None, "gx"), P(None, ("gx", "gy"), None, None)),
        check_vma=False,
    )
```
